32 devices in a mesh: groups: 2 (over y), wide: 4 (over z), slab: 2 (over x), sub: 2 (over core).
Axes of the slice: x: 2, y: 2, z: 4, core: 2. Of those that a mesh axis runs over, the one named last changes fastest.
Arguments:
- source: bfloat16 [16, 64, 2, 32, 128], P(('groups', 'slab'), 'wide', None, 'sub'), parts along dimension 0, may hold values from -6 to 6
- aggregation: bfloat16 [2, 1024, 128], P(None, 'groups'), parts along dimension 1, may hold values from -0.375 to 0.375
- translators: bfloat16 [2, 1024, 31, 255], P(None, ('groups', 'wide')), parts along dimension 1, may hold values from -0.1875 to 0.1875
- tile_map: int32 [8, 8], replicated, may hold values from 0 to 30, as said below
- far_mask: int32 [8, 8], replicated, may hold values from 0 to 1
- box_offsets: int32 [64, 64], replicated, may hold values from 0 to 254, as said below
- disaggregation: bfloat16 [2, 128, 1024], P(None, None, 'groups'), parts along dimension 2, may hold values from -0.1875 to 0.1875
Outputs:
- field: bfloat16 [16, 64, 2, 32, 128], P(('groups', 'slab'), 'wide', None, 'sub'), parts along dimension 0
The draws below stay inside these ranges and needn't reach their ends.
There are 2 independent parts, one for each index of `groups`. The reference program is written for one: setup_inputs(seed, part) draws one part's arguments, and reference() takes and returns one part's arrays. A program takes and returns all parts, laid end to end along the dimension named above; an argument that names none is the same for every part. Nothing has to cross between parts.
Inputs may be any that keep to these rules, and one draw needn't show every extreme that they name: tile_map[a, c] = row[a] - row[c] + 16 - 1, where row holds the distinct grid rows of the rows of boxes in increasing order, row[0] = 0 and row[last] = 16 - 1; far_mask[a, c] = 1 exactly where |row[a] - row[c]| >= 2. `box_offsets`: offset index of a pair of boxes of one row.
All inputs are finite; a program needn't handle non-finite values.
Results may differ from the reference program's by a relative error of at most 0.0058.
Values may be sent and summed in bfloat16 or wider, within the bound.
No kernel may reach another device: no remote copies, remote signals or barrier semaphores. Data moves between devices by JAX's collectives and lax.ppermute only.
A program may use at most 192 MiB of HBM per device.

```python
import jax
import jax.numpy as jnp
from jax import lax

P_SIZE = 128
K = 512
R = 32
COLS = 64
ROWS = 8
GY = 16
GX = 128
NTRANS = 31
NOFF = 255


def grid_positions(key, number, extent):
    middle = jax.random.permutation(key, extent - 2)[:number - 2].astype(jnp.int32) + 1
    extremes = jnp.array([0, extent - 1], dtype=jnp.int32)
    return jnp.sort(jnp.concatenate([extremes, middle]))


def row_positions(key):
    return grid_positions(jax.random.fold_in(key, 1), ROWS, GY)


def draw_tile_map(key, part):
    rows_at = row_positions(key)
    return (rows_at[:, None] - rows_at[None, :] + GY - 1).astype(jnp.int32)


def draw_far_mask(key, part):
    rows_at = row_positions(key)
    return (jnp.abs(rows_at[:, None] - rows_at[None, :]) >= 2).astype(jnp.int32)


def draw_box_offsets(key, part):
    cols_at = grid_positions(jax.random.fold_in(key, 2), COLS, GX)
    return (cols_at[:, None] - cols_at[None, :] + GX - 1).astype(jnp.int32)


def block_levels(rng, dims, cuts, least, top_value):
    gain = 1.0
    for dim, blocks in cuts:
        draws = jax.random.uniform(jax.random.fold_in(jax.random.fold_in(rng, 6), dim), (blocks,), jnp.float32, least / len(cuts), top_value / len(cuts))
        gain = gain * jnp.repeat(jnp.exp(draws), dims[dim] // blocks).reshape((-1,) + (1,) * (len(dims) - 1 - dim))
    return gain


def normal_values(key, shape, scale, most, shards=(), kind=jnp.bfloat16):
    gain = block_levels(key, shape, shards, -0.22, 0.18) if shards else 1.0
    entries = jax.random.normal(key, shape, jnp.float32) * scale * gain
    return jnp.minimum(jnp.maximum(entries, -most), most).astype(kind)


def setup_inputs(seed: int = 0, part: int = 0) -> dict:
    key_of = jax.random.split(jax.random.key(seed), 8)
    own_keys = jax.random.split(jax.random.fold_in(key_of[7], part), 8)
    source = normal_values(own_keys[0], (ROWS, COLS, 2, R, P_SIZE), 1.0, 6.0, ((0, 2), (1, 4), (3, 2)))
    aggregation = normal_values(own_keys[1], (2, K, P_SIZE), (2 * P_SIZE) ** -0.5, 0.375)
    translators = normal_values(own_keys[2], (2, K, NTRANS, NOFF), (2 * ROWS * COLS) ** -0.5, 0.1875, ((1, 4),))
    tile_map = draw_tile_map(jax.random.fold_in(key_of[7], 71), part)
    far_mask = draw_far_mask(jax.random.fold_in(key_of[7], 71), part)
    box_offsets = draw_box_offsets(jax.random.fold_in(key_of[7], 71), part)
    disaggregation = normal_values(own_keys[6], (2, P_SIZE, K), (2 * K) ** -0.5, 0.1875)
    return {"source": source, "aggregation": aggregation, "translators": translators, "tile_map": tile_map, "far_mask": far_mask, "box_offsets": box_offsets, "disaggregation": disaggregation}


def complex_product(form, first_real, first_imag, second_real, second_imag):
    real_part = jnp.einsum(form, first_real, second_real) - jnp.einsum(form, first_imag, second_imag)
    imag_part = jnp.einsum(form, first_real, second_imag) + jnp.einsum(form, first_imag, second_real)
    return real_part, imag_part


def reference(source, aggregation, translators, tile_map, far_mask, box_offsets, disaggregation):
    widened = source.astype(jnp.float32)
    pattern = aggregation.astype(jnp.float32)
    out_real, out_imag = complex_product("axrp,kp->axkr", widened[:, :, 0], widened[:, :, 1], pattern[0], pattern[1])
    outgoing = jnp.stack([out_real, out_imag], 0).astype(jnp.bfloat16)
    outgoing = lax.optimization_barrier(outgoing).astype(jnp.float32)
    tile_count = NTRANS * NOFF
    pair_index = jnp.where(far_mask[:, None, :, None] == 1,
                           tile_map[:, None, :, None] * NOFF + box_offsets[None, :, None, :],
                           tile_count).astype(jnp.int32)
    table = translators.astype(jnp.float32).reshape(2, K, tile_count)
    table = jnp.concatenate([table, jnp.zeros((2, K, 1), jnp.float32)], axis=2)
    block_size = 8

    def one_block(block_index):
        first = (block_index * block_size).astype(jnp.int32)
        sub_table = lax.dynamic_slice_in_dim(table, first, block_size, 1)
        coupling = jnp.take(sub_table, pair_index, axis=2)
        sources = lax.dynamic_slice_in_dim(outgoing, first, block_size, 3)
        parts = complex_product("kaxcy,cykr->kaxr", coupling[0], coupling[1], sources[0], sources[1])
        return jnp.stack(parts, 0)

    blocks = lax.map(one_block, jnp.arange(K // block_size, dtype=jnp.int32))
    incoming = jnp.moveaxis(blocks, 0, 1).reshape(2, K, ROWS, COLS, R).astype(jnp.bfloat16)
    incoming = lax.optimization_barrier(incoming).astype(jnp.float32)
    receive = disaggregation.astype(jnp.float32)
    field_real, field_imag = complex_product("kaxr,pk->axrp", incoming[0], incoming[1], receive[0], receive[1])
    return jnp.stack([field_real, field_imag], axis=2).astype(jnp.bfloat16)
```

```python
import functools

import jax
import jax.numpy as jnp
from jax import lax
from jax.experimental import pallas as pl
from jax.experimental.pallas import tpu as pltpu
from jax.sharding import PartitionSpec as P

OWNERS = ("wide", "slab", "sub")
LANES = 128
VMEM = 56 * 1024 * 1024
NT = (((1,), (1,)), ((), ()))
TN = (((0,), (0,)), ((), ()))


def outgoing_kernel(boxes, illum, devices, half, src_ref, agg_ref, out_ref, wide_src, wide_out):
    unknowns = src_ref.shape[1]
    wide_src[...] = src_ref[...].astype(jnp.float32)
    real = agg_ref[0].astype(jnp.float32)
    imag = agg_ref[1].astype(jnp.float32)

    def pick(array, part):
        return jnp.concatenate(
            [array[(2 * d + part) * half:(2 * d + part + 1) * half] for d in range(devices)], axis=0
        )

    real_low, real_high = pick(real, 0), pick(real, 1)
    imag_low, imag_high = pick(imag, 0), pick(imag, 1)
    to_real = jnp.concatenate([real_low, -imag_low, real_high, -imag_high], axis=1).astype(jnp.bfloat16)
    to_imag = jnp.concatenate([imag_low, real_low, imag_high, real_high], axis=1).astype(jnp.bfloat16)
    zeros = jnp.zeros((boxes, 2 * unknowns), jnp.bfloat16)
    rows = devices * half
    for r in range(illum):
        both = jnp.concatenate(
            [wide_src[pl.ds(q * illum + r, boxes, stride=2 * illum), :] for q in range(2)], axis=1
        ).astype(jnp.bfloat16)
        right = jnp.concatenate(
            [jnp.concatenate([both, zeros], axis=1), jnp.concatenate([zeros, both], axis=1)], axis=0
        )
        for q, left in ((0, to_real), (1, to_imag)):
            wide_out[pl.ds(q * illum + r, rows, stride=2 * illum), :] = lax.dot_general(
                left, right, NT, preferred_element_type=jnp.float32
            )
    out_ref[...] = wide_out[...].astype(jnp.bfloat16)


def expand_kernel(middle, base_ref, index_ref, table_ref, out_ref, wide_table):
    translators, offsets = table_ref.shape[2], table_ref.shape[3]
    groups = index_ref.shape[0] // 8
    for q in range(2):
        wide_table[q, :, 0:LANES] = table_ref[q, 0, :, 0:LANES].astype(jnp.float32)
        wide_table[q, :, LANES:offsets] = table_ref[q, 0, :, LANES:offsets].astype(jnp.float32)
    index = [index_ref[8 * g:8 * g + 8, :] for g in range(groups)]
    upper = [i >= LANES for i in index]
    lane = [i & (LANES - 1) for i in index]
    out_ref[0, middle] = jnp.zeros(out_ref.shape[2:], jnp.bfloat16)
    for t in range(translators):
        if abs(t - middle) < 2:
            continue
        for q in range(2):
            low = jnp.broadcast_to(wide_table[q, t:t + 1, 0:LANES], (8, LANES))
            high = jnp.broadcast_to(wide_table[q, t:t + 1, LANES:2 * LANES], (8, LANES))
            tiles = [
                jnp.where(
                    upper[g],
                    jnp.take_along_axis(high, lane[g], axis=1),
                    jnp.take_along_axis(low, lane[g], axis=1),
                )
                for g in range(groups)
            ]
            out_ref[0, t, :, q * LANES:(q + 1) * LANES] = jnp.concatenate(tiles, axis=0).astype(
                jnp.bfloat16
            )


def translate_kernel(wide, slab, sub, rows, columns, pair_ref, src_ref, exp_ref, out_ref):
    illum = src_ref.shape[3]
    all_rows = slab * rows
    x_half = exp_ref.shape[3]
    per_half = x_half // columns
    lane = lax.broadcasted_iota(jnp.int32, (illum, LANES), 1)
    group = lane // columns
    lower = lane < LANES // 2
    zero = jnp.zeros((illum, LANES), jnp.float32)
    sums = [None, None]
    turned = {}

    def turn(s, u, q, w, amount):
        key = (s, u, q, w, amount)
        if key not in turned:
            tile = src_ref[(w * slab + s) * sub + u, 0, q].astype(jnp.float32)
            turned[key] = pltpu.roll(tile, amount * columns, 1) if amount else tile
        return turned[key]

    groups = LANES // columns
    for c in range(all_rows):
        s, own = c // rows, c % rows
        for k2 in range(2):
            position = k2 * rows + own
            parts = {}
            for u in range(sub):
                for q in range(2):
                    for h in range(2):
                        tile = zero
                        for w in range(wide):
                            place = h * wide + w
                            tile = jnp.where(
                                group == place, turn(s, u, q, w, (place - position) % groups), tile
                            )
                        parts[u, q, h] = tile
            left = []
            for h in range(2):
                for u in range(sub):
                    left.append(jnp.concatenate([parts[u, 0, h], -parts[u, 1, h]], axis=1))
                    left.append(jnp.concatenate([parts[u, 1, h], parts[u, 0, h]], axis=1))
            left = jnp.concatenate(left, axis=0).astype(jnp.bfloat16)
            right = jnp.concatenate(
                [
                    exp_ref[k2, 0, pair_ref[a * all_rows + c], v * columns:(v + 1) * columns, :]
                    for v in range(per_half)
                    for a in range(all_rows)
                ],
                axis=0,
            )
            product = lax.dot_general(left, right, NT, preferred_element_type=jnp.float32)
            sums[k2] = product if sums[k2] is None else sums[k2] + product
    for h in range(2):
        for u in range(sub):
            for q in range(2):
                row = ((h * sub + u) * 2 + q) * illum
                for v in range(per_half):
                    first = sums[0][row:row + illum, v * LANES:(v + 1) * LANES]
                    second = sums[1][row:row + illum, v * LANES:(v + 1) * LANES]
                    for s in range(slab):
                        if s == 0:
                            tile = jnp.where(lower, first, pltpu.roll(second, LANES // 2, 1))
                        else:
                            tile = jnp.where(lower, pltpu.roll(first, LANES // 2, 1), second)
                        w = h * per_half + v
                        out_ref[(w * slab + s) * sub + u, 0, q] = tile.astype(jnp.bfloat16)


def field_kernel(boxes, illum, devices, half, inc_ref, dis_ref, out_ref, wide_inc, wide_out):
    wide_inc[...] = inc_ref[...].astype(jnp.float32)
    real = dis_ref[0].astype(jnp.float32).T
    imag = dis_ref[1].astype(jnp.float32).T

    def pick(array, part):
        return jnp.concatenate(
            [array[(2 * d + part) * half:(2 * d + part + 1) * half] for d in range(devices)], axis=0
        )

    sides = []
    for part in range(2):
        real_part, imag_part = pick(real, part), pick(imag, part)
        sides.append(
            jnp.concatenate(
                [
                    jnp.concatenate([real_part, imag_part], axis=1),
                    jnp.concatenate([-imag_part, real_part], axis=1),
                ],
                axis=0,
            )
        )
    right = jnp.concatenate(sides, axis=1).astype(jnp.bfloat16)
    unknowns = out_ref.shape[1]
    rows = devices * half
    for r in range(illum):
        left = jnp.concatenate(
            [wide_inc[pl.ds(q * illum + r, rows, stride=2 * illum), :] for q in range(2)], axis=0
        ).astype(jnp.bfloat16)
        product = lax.dot_general(left, right, TN, preferred_element_type=jnp.float32)
        total = product[:boxes, :2 * unknowns] + product[boxes:, 2 * unknowns:]
        for q in range(2):
            wide_out[pl.ds(q * illum + r, boxes, stride=2 * illum), :] = total[
                :, q * unknowns:(q + 1) * unknowns
            ]
    out_ref[...] = wide_out[...].astype(jnp.bfloat16)


def tiled_local(wide, slab, sub, source, aggregation, translators, tile_map, far_mask, box_offsets, disaggregation):
    rows, columns, _, illum, unknowns = source.shape
    devices = wide * slab * sub
    directions = aggregation.shape[1]
    half = directions // devices // 2
    boxes = rows * columns
    all_rows = slab * rows
    count = translators.shape[2]
    offsets = translators.shape[3]
    middle = count // 2
    params = pltpu.CompilerParams(vmem_limit_bytes=VMEM)

    lines = devices * half * 2 * illum
    outgoing = pl.pallas_call(
        functools.partial(outgoing_kernel, boxes, illum, devices, half),
        out_shape=jax.ShapeDtypeStruct((lines, LANES), jnp.bfloat16),
        scratch_shapes=[
            pltpu.VMEM((boxes * 2 * illum, unknowns), jnp.float32),
            pltpu.VMEM((lines, LANES), jnp.float32),
        ],
        compiler_params=params,
        name="outgoing",
    )(source.reshape(boxes * 2 * illum, unknowns), aggregation)
    block = (devices, half, 2, illum, LANES)
    received = lax.all_to_all(outgoing.reshape(block), OWNERS, split_axis=0, concat_axis=0, tiled=True)

    side = box_offsets.shape[0]
    x_half = side // 2
    index = jnp.concatenate([box_offsets[:x_half], box_offsets[x_half:]], axis=1)
    base = lax.axis_index("slab") * sub + lax.axis_index("sub")
    expanded = pl.pallas_call(
        functools.partial(expand_kernel, middle),
        grid_spec=pltpu.PrefetchScalarGridSpec(
            num_scalar_prefetch=1,
            grid=(2 * half,),
            in_specs=[
                pl.BlockSpec((x_half, 2 * side), lambda k, base: (0, 0)),
                pl.BlockSpec((2, 1, count, offsets), lambda k, base: (0, base[0] * 2 * half + k, 0, 0)),
            ],
            out_specs=pl.BlockSpec((1, count, x_half, 2 * LANES), lambda k, base: (k, 0, 0, 0)),
            scratch_shapes=[pltpu.VMEM((2, count, 2 * LANES), jnp.float32)],
        ),
        out_shape=jax.ShapeDtypeStruct((2 * half, count, x_half, 2 * LANES), jnp.bfloat16),
        compiler_params=params,
        name="expand",
    )(base.reshape(1), index, translators)

    pairs = jnp.where(far_mask == 1, tile_map, middle).reshape(-1)
    incoming = pl.pallas_call(
        functools.partial(translate_kernel, wide, slab, sub, rows, columns),
        grid_spec=pltpu.PrefetchScalarGridSpec(
            num_scalar_prefetch=1,
            grid=(half,),
            in_specs=[
                pl.BlockSpec((devices, 1, 2, illum, LANES), lambda k, pairs: (0, k, 0, 0, 0)),
                pl.BlockSpec((2, 1, count, x_half, 2 * LANES), lambda k, pairs: (0, k, 0, 0, 0)),
            ],
            out_specs=pl.BlockSpec((devices, 1, 2, illum, LANES), lambda k, pairs: (0, k, 0, 0, 0)),
        ),
        out_shape=jax.ShapeDtypeStruct(block, jnp.bfloat16),
        compiler_params=params,
        name="translate",
    )(pairs, received, expanded.reshape(2, half, count, x_half, 2 * LANES))

    returned = lax.all_to_all(incoming, OWNERS, split_axis=0, concat_axis=0, tiled=True)
    field = pl.pallas_call(
        functools.partial(field_kernel, boxes, illum, devices, half),
        out_shape=jax.ShapeDtypeStruct((boxes * 2 * illum, unknowns), jnp.bfloat16),
        scratch_shapes=[
            pltpu.VMEM((lines, LANES), jnp.float32),
            pltpu.VMEM((boxes * 2 * illum, unknowns), jnp.float32),
        ],
        compiler_params=params,
        name="field",
    )(returned.reshape(lines, LANES), disaggregation)
    return field.reshape(source.shape)


def aggregate(values, pattern_real, pattern_imag):

    def product(left_side, right_side):
        return jnp.einsum(
            "axrp,kp->krax", left_side, right_side, preferred_element_type=jnp.float32
        )

    values_real = values[:, :, 0]
    values_imag = values[:, :, 1]
    out_real = product(values_real, pattern_real) - product(values_imag, pattern_imag)
    out_imag = product(values_real, pattern_imag) + product(values_imag, pattern_real)
    return jnp.stack([out_real, out_imag], axis=1).astype(jnp.bfloat16)


def general_local(source, aggregation, translators, tile_map, far_mask, box_offsets, disaggregation):
    own_rows = source.shape[0]
    tile_count = translators.shape[2]
    offset_count = translators.shape[3]
    box_count = box_offsets.shape[0]
    target_block = 2
    block_count = own_rows // target_block
    outgoing = lax.all_to_all(
        aggregate(source, aggregation[0], aggregation[1]),
        "wide",
        split_axis=0,
        concat_axis=4,
        tiled=True,
    )
    directions_here = outgoing.shape[0]
    illum_here = outgoing.shape[2]
    row_table = jnp.concatenate(
        [translators, jnp.zeros((2, directions_here, 1, offset_count), jnp.bfloat16)], axis=2
    )
    offset_ids = lax.broadcasted_iota(jnp.int32, (offset_count, box_count, box_count), 0)
    selector = (offset_ids == box_offsets[None, :, :]).astype(jnp.bfloat16)
    selector = selector.reshape(offset_count, box_count * box_count)

    def translate(target_first, source_first, source_block):
        source_count = source_block.shape[3]
        pair_map = lax.dynamic_slice(
            tile_map, (target_first, source_first), (target_block, source_count)
        )
        pair_far = lax.dynamic_slice(
            far_mask, (target_first, source_first), (target_block, source_count)
        )
        pair_index = jnp.where(pair_far == 1, pair_map, tile_count)
        pair_rows = jnp.take(row_table, pair_index.reshape(-1), axis=2)
        expanded = jnp.dot(
            pair_rows.reshape(-1, offset_count), selector, preferred_element_type=jnp.float32
        )
        coupling = expanded.astype(jnp.bfloat16).reshape(
            2, directions_here, target_block, source_count, box_count, box_count
        )
        values = source_block.reshape(directions_here, 2 * illum_here, source_count, box_count)
        combos = jnp.einsum(
            "klcy,qkacxy->klqax", values, coupling, preferred_element_type=jnp.float32
        )
        combos = combos.reshape(directions_here, 2, illum_here, 2, target_block * box_count)
        incoming_real = combos[:, 0, :, 0] - combos[:, 1, :, 1]
        incoming_imag = combos[:, 1, :, 0] + combos[:, 0, :, 1]
        return jnp.stack([incoming_real, incoming_imag], axis=1)

    slab_first = lax.axis_index("slab") * own_rows

    def block_rows(block_index):
        return translate(block_index * target_block, slab_first, outgoing)

    summed = lax.psum_scatter(
        lax.map(block_rows, jnp.arange(block_count * lax.axis_size("slab"), dtype=jnp.int32)),
        "slab",
        scatter_dimension=0,
        tiled=True,
    )
    incoming = summed.astype(jnp.bfloat16)
    incoming = incoming.reshape(incoming.shape[:4] + (target_block, box_count))
    item_rows = lax.all_to_all(incoming, "wide", split_axis=5, concat_axis=1, tiled=True)

    def product(left_side, right_side):
        return jnp.einsum(
            "bkrax,pk->baxrp", left_side, right_side, preferred_element_type=jnp.float32
        )

    items_real = item_rows[:, :, 0]
    items_imag = item_rows[:, :, 1]
    field_real = product(items_real, disaggregation[0]) - product(items_imag, disaggregation[1])
    field_imag = product(items_real, disaggregation[1]) + product(items_imag, disaggregation[0])
    stacked = jnp.stack([field_real, field_imag], axis=3).astype(jnp.bfloat16)
    return stacked.reshape((stacked.shape[0] * stacked.shape[1],) + stacked.shape[2:])


def local(wide, slab, sub, *args):
    source, aggregation, translators, _, _, box_offsets, _ = args
    rows, columns, _, illum, unknowns = source.shape
    share = aggregation.shape[1] // (wide * slab * sub)
    tiles = (
        2 * rows * columns == LANES
        and 2 * box_offsets.shape[0] == LANES
        and columns * wide == box_offsets.shape[0]
        and slab == 2
        and columns == 16
        and illum == 16
        and share % 32 == 0
        and unknowns == LANES
        and LANES < translators.shape[3] <= 2 * LANES
    )
    if tiles:
        return tiled_local(wide, slab, sub, *args)
    return general_local(*args)


def solution(mesh):
    placed = (
        P(("groups", "slab"), "wide", None, "sub", None),
        P(None, "groups", None),
        P(None, ("groups", "wide"), None, None),
        P(),
        P(),
        P(),
        P(None, None, "groups"),
    )
    return jax.shard_map(
        functools.partial(local, mesh.shape["wide"], mesh.shape["slab"], mesh.shape["sub"]),
        mesh=mesh,
        in_specs=placed,
        out_specs=P(("groups", "slab"), "wide", None, "sub", None),
        check_vma=False,
    )
```

```python
import functools

import jax
import jax.numpy as jnp
from jax import lax
from jax.experimental import pallas as pl
from jax.experimental.pallas import tpu as pltpu
from jax.sharding import PartitionSpec as P

OWNERS = ("wide", "slab", "sub")
LANES = 128
VMEM = 56 * 1024 * 1024
NT = (((1,), (1,)), ((), ()))
TN = (((0,), (0,)), ((), ()))


def outgoing_kernel(boxes, illum, devices, half, src_ref, agg_ref, out_ref, wide_src, wide_out):
    unknowns = src_ref.shape[1]
    wide_src[...] = src_ref[...].astype(jnp.float32)
    real = agg_ref[0].astype(jnp.float32)
    imag = agg_ref[1].astype(jnp.float32)

    def pick(array, part):
        return jnp.concatenate(
            [array[(2 * d + part) * half:(2 * d + part + 1) * half] for d in range(devices)], axis=0
        )

    real_low, real_high = pick(real, 0), pick(real, 1)
    imag_low, imag_high = pick(imag, 0), pick(imag, 1)
    to_real = jnp.concatenate([real_low, -imag_low, real_high, -imag_high], axis=1).astype(jnp.bfloat16)
    to_imag = jnp.concatenate([imag_low, real_low, imag_high, real_high], axis=1).astype(jnp.bfloat16)
    zeros = jnp.zeros((boxes, 2 * unknowns), jnp.bfloat16)
    rows = devices * half
    for r in range(illum):
        both = jnp.concatenate(
            [wide_src[pl.ds(q * illum + r, boxes, stride=2 * illum), :] for q in range(2)], axis=1
        ).astype(jnp.bfloat16)
        right = jnp.concatenate(
            [jnp.concatenate([both, zeros], axis=1), jnp.concatenate([zeros, both], axis=1)], axis=0
        )
        for q, left in ((0, to_real), (1, to_imag)):
            wide_out[pl.ds(q * illum + r, rows, stride=2 * illum), :] = lax.dot_general(
                left, right, NT, preferred_element_type=jnp.float32
            )
    out_ref[...] = wide_out[...].astype(jnp.bfloat16)


def expand_kernel(middle, base_ref, index_ref, table_ref, out_ref, wide_table):
    translators, offsets = table_ref.shape[2], table_ref.shape[3]
    groups = index_ref.shape[0] // 8
    for q in range(2):
        wide_table[q, :, 0:LANES] = table_ref[q, 0, :, 0:LANES].astype(jnp.float32)
        wide_table[q, :, LANES:offsets] = table_ref[q, 0, :, LANES:offsets].astype(jnp.float32)
    index = [index_ref[8 * g:8 * g + 8, :] for g in range(groups)]
    upper = [i >= LANES for i in index]
    lane = [i & (LANES - 1) for i in index]
    per_side = groups // 2
    for v in range(2):
        out_ref[v, 0, middle] = jnp.zeros(out_ref.shape[3:], jnp.bfloat16)
    for t in range(translators):
        if abs(t - middle) < 2:
            continue
        for q in range(2):
            low = jnp.broadcast_to(wide_table[q, t:t + 1, 0:LANES], (8, LANES))
            high = jnp.broadcast_to(wide_table[q, t:t + 1, LANES:2 * LANES], (8, LANES))
            tiles = [
                jnp.where(
                    upper[g],
                    jnp.take_along_axis(high, lane[g], axis=1),
                    jnp.take_along_axis(low, lane[g], axis=1),
                )
                for g in range(groups)
            ]
            for v in range(2):
                out_ref[v, 0, t, :, q * LANES:(q + 1) * LANES] = jnp.concatenate(
                    tiles[v * per_side:(v + 1) * per_side], axis=0
                ).astype(jnp.bfloat16)


def translate_kernel(wide, slab, sub, rows, columns, pair_ref, src_ref, exp_ref, out_ref):
    illum = src_ref.shape[3]
    steps = exp_ref.shape[2]
    all_rows = slab * rows
    lane = lax.broadcasted_iota(jnp.int32, (illum, LANES), 1)
    group = lane // columns
    groups = LANES // columns
    lower = lane < LANES // 2
    zero = jnp.zeros((illum, LANES), jnp.float32)
    for step in range(steps):
        here = pl.program_id(0) * steps + step
        sums = [None, None]
        turned = {}

        def turn(s, u, q, w, amount):
            key = (s, u, q, w, amount)
            if key not in turned:
                tile = src_ref[(w * slab + s) * sub + u, here, q].astype(jnp.float32)
                turned[key] = pltpu.roll(tile, amount * columns, 1) if amount else tile
            return turned[key]

        for c in range(all_rows):
            s, own = c // rows, c % rows
            for k2 in range(2):
                position = k2 * rows + own
                parts = {}
                for u in range(sub):
                    for q in range(2):
                        for h in range(2):
                            tile = zero
                            for w in range(wide):
                                place = h * wide + w
                                tile = jnp.where(
                                    group == place,
                                    turn(s, u, q, w, (place - position) % groups),
                                    tile,
                                )
                            parts[u, q, h] = tile
                left = []
                for h in range(2):
                    for u in range(sub):
                        left.append(jnp.concatenate([parts[u, 0, h], -parts[u, 1, h]], axis=1))
                        left.append(jnp.concatenate([parts[u, 1, h], parts[u, 0, h]], axis=1))
                left = jnp.concatenate(left, axis=0).astype(jnp.bfloat16)
                right = jnp.concatenate(
                    [exp_ref[0, k2, step, pair_ref[a * all_rows + c]] for a in range(all_rows)], axis=0
                )
                product = lax.dot_general(left, right, NT, preferred_element_type=jnp.float32)
                sums[k2] = product if sums[k2] is None else sums[k2] + product
        for h in range(2):
            for u in range(sub):
                for q in range(2):
                    row = ((h * sub + u) * 2 + q) * illum
                    first = sums[0][row:row + illum]
                    second = sums[1][row:row + illum]
                    for s in range(slab):
                        if s == 0:
                            tile = jnp.where(lower, first, pltpu.roll(second, LANES // 2, 1))
                        else:
                            tile = jnp.where(lower, pltpu.roll(first, LANES // 2, 1), second)
                        out_ref[(h * slab + s) * sub + u, here, q] = tile.astype(jnp.bfloat16)


def field_kernel(boxes, illum, devices, half, side_ref, inc_ref, dis_ref, out_ref, wide_inc, wide_out):
    wide_inc[...] = inc_ref[...].astype(jnp.float32)
    real = dis_ref[0].astype(jnp.float32).T
    imag = dis_ref[1].astype(jnp.float32).T

    def pick(array, part):
        return jnp.concatenate(
            [array[(2 * d + part) * half:(2 * d + part + 1) * half] for d in range(devices)], axis=0
        )

    sides = []
    for part in range(2):
        real_part, imag_part = pick(real, part), pick(imag, part)
        sides.append(
            jnp.concatenate(
                [
                    jnp.concatenate([real_part, imag_part], axis=1),
                    jnp.concatenate([-imag_part, real_part], axis=1),
                ],
                axis=0,
            )
        )
    right = jnp.concatenate(sides, axis=1).astype(jnp.bfloat16)
    unknowns = out_ref.shape[1]
    rows = devices * half
    for r in range(illum):
        left = jnp.concatenate(
            [wide_inc[pl.ds(q * illum + r, rows, stride=2 * illum), :] for q in range(2)], axis=0
        ).astype(jnp.bfloat16)
        product = lax.dot_general(left, right, TN, preferred_element_type=jnp.float32)
        total = product[:boxes, :2 * unknowns] + product[boxes:, 2 * unknowns:]
        for q in range(2):
            wide_out[pl.ds(q * illum + r, boxes, stride=2 * illum), :] = total[
                :, q * unknowns:(q + 1) * unknowns
            ]
    out_ref[...] = wide_out[...].astype(out_ref.dtype)


def tiled_local(wide, slab, sub, source, aggregation, translators, tile_map, far_mask, box_offsets, disaggregation):
    rows, columns, _, illum, unknowns = source.shape
    devices = wide * slab * sub
    directions = aggregation.shape[1]
    half = directions // devices // 2
    boxes = rows * columns
    all_rows = slab * rows
    count = translators.shape[2]
    offsets = translators.shape[3]
    middle = count // 2
    params = pltpu.CompilerParams(vmem_limit_bytes=VMEM)

    lines = devices * half * 2 * illum
    outgoing = pl.pallas_call(
        functools.partial(outgoing_kernel, boxes, illum, devices, half),
        out_shape=jax.ShapeDtypeStruct((lines, LANES), jnp.bfloat16),
        scratch_shapes=[
            pltpu.VMEM((boxes * 2 * illum, unknowns), jnp.float32),
            pltpu.VMEM((lines, LANES), jnp.float32),
        ],
        compiler_params=params,
        name="outgoing",
    )(source.reshape(boxes * 2 * illum, unknowns), aggregation)
    block = (devices, half, 2, illum, LANES)
    received = lax.all_to_all(outgoing.reshape(block), OWNERS, split_axis=0, concat_axis=0, tiled=True)

    side = box_offsets.shape[0]
    x_half = side // 2
    place = lax.axis_index("wide") // 2
    by_side = jnp.where(place == 0, jnp.roll(box_offsets, x_half, axis=0), box_offsets)
    by_side = by_side.reshape(2, 2, columns, side)
    index = jnp.concatenate([by_side[:, 0], by_side[:, 1]], axis=-1).reshape(x_half, 2 * side)
    base = lax.axis_index("slab") * sub + lax.axis_index("sub")
    expanded = pl.pallas_call(
        functools.partial(expand_kernel, middle),
        grid_spec=pltpu.PrefetchScalarGridSpec(
            num_scalar_prefetch=1,
            grid=(2 * half,),
            in_specs=[
                pl.BlockSpec((x_half, 2 * side), lambda k, base: (0, 0)),
                pl.BlockSpec((2, 1, count, offsets), lambda k, base: (0, base[0] * 2 * half + k, 0, 0)),
            ],
            out_specs=pl.BlockSpec((2, 1, count, columns, 2 * LANES), lambda k, base: (0, k, 0, 0, 0)),
            scratch_shapes=[pltpu.VMEM((2, count, 2 * LANES), jnp.float32)],
        ),
        out_shape=jax.ShapeDtypeStruct((2, 2 * half, count, columns, 2 * LANES), jnp.bfloat16),
        compiler_params=params,
        name="expand",
    )(base.reshape(1), index, translators)
    expanded = expanded.reshape(2, 2, half, count, columns, 2 * LANES)

    pairs = jnp.where(far_mask == 1, tile_map, middle).reshape(-1)
    near = devices // 2
    lines = lines // 2
    shape = (boxes * 2 * illum, unknowns)
    neighbours = [[first * near + d for d in range(near)] for first in range(2)]
    steps = 2

    def translate(v):
        return pl.pallas_call(
            functools.partial(translate_kernel, wide, slab, sub, rows, columns),
            grid_spec=pltpu.PrefetchScalarGridSpec(
                num_scalar_prefetch=1,
                grid=(half // steps,),
                in_specs=[
                    pl.BlockSpec(block, lambda k, pairs: (0, 0, 0, 0, 0)),
                    pl.BlockSpec(
                        (1, 2, steps, count, columns, 2 * LANES), lambda k, pairs: (v, 0, k, 0, 0, 0)
                    ),
                ],
                out_specs=pl.BlockSpec((near,) + block[1:], lambda k, pairs: (0, 0, 0, 0, 0)),
            ),
            out_shape=jax.ShapeDtypeStruct((near,) + block[1:], jnp.bfloat16),
            compiler_params=params,
            name="translate",
        )(pairs, received, expanded)

    def exchange(values):
        return lax.all_to_all(
            values, OWNERS, split_axis=0, concat_axis=0, tiled=True, axis_index_groups=neighbours
        )

    def field(values, kind):
        return pl.pallas_call(
            functools.partial(field_kernel, boxes, illum, near, half),
            grid_spec=pltpu.PrefetchScalarGridSpec(
                num_scalar_prefetch=1,
                grid=(1,),
                in_specs=[
                    pl.BlockSpec((lines, LANES), lambda i, place: (0, 0)),
                    pl.BlockSpec((2, unknowns, directions // 2), lambda i, place: (0, 0, place[0])),
                ],
                out_specs=pl.BlockSpec(shape, lambda i, place: (0, 0)),
                scratch_shapes=[pltpu.VMEM((lines, LANES), jnp.float32), pltpu.VMEM(shape, jnp.float32)],
            ),
            out_shape=jax.ShapeDtypeStruct(shape, kind),
            compiler_params=params,
            name="field",
        )(place.reshape(1), values.reshape(lines, LANES), disaggregation)

    far_half = exchange(translate(0))
    near_half = exchange(translate(1))
    across = lax.ppermute(
        field(far_half, jnp.bfloat16), "wide", [(w, (w + wide // 2) % wide) for w in range(wide)]
    )
    total = field(near_half, jnp.float32) + across.astype(jnp.float32)
    return total.astype(jnp.bfloat16).reshape(source.shape)


def aggregate(values, pattern_real, pattern_imag):

    def product(left_side, right_side):
        return jnp.einsum(
            "axrp,kp->krax", left_side, right_side, preferred_element_type=jnp.float32
        )

    values_real = values[:, :, 0]
    values_imag = values[:, :, 1]
    out_real = product(values_real, pattern_real) - product(values_imag, pattern_imag)
    out_imag = product(values_real, pattern_imag) + product(values_imag, pattern_real)
    return jnp.stack([out_real, out_imag], axis=1).astype(jnp.bfloat16)


def general_local(source, aggregation, translators, tile_map, far_mask, box_offsets, disaggregation):
    own_rows = source.shape[0]
    tile_count = translators.shape[2]
    offset_count = translators.shape[3]
    box_count = box_offsets.shape[0]
    target_block = 2
    block_count = own_rows // target_block
    outgoing = lax.all_to_all(
        aggregate(source, aggregation[0], aggregation[1]),
        "wide",
        split_axis=0,
        concat_axis=4,
        tiled=True,
    )
    directions_here = outgoing.shape[0]
    illum_here = outgoing.shape[2]
    row_table = jnp.concatenate(
        [translators, jnp.zeros((2, directions_here, 1, offset_count), jnp.bfloat16)], axis=2
    )
    offset_ids = lax.broadcasted_iota(jnp.int32, (offset_count, box_count, box_count), 0)
    selector = (offset_ids == box_offsets[None, :, :]).astype(jnp.bfloat16)
    selector = selector.reshape(offset_count, box_count * box_count)

    def translate(target_first, source_first, source_block):
        source_count = source_block.shape[3]
        pair_map = lax.dynamic_slice(
            tile_map, (target_first, source_first), (target_block, source_count)
        )
        pair_far = lax.dynamic_slice(
            far_mask, (target_first, source_first), (target_block, source_count)
        )
        pair_index = jnp.where(pair_far == 1, pair_map, tile_count)
        pair_rows = jnp.take(row_table, pair_index.reshape(-1), axis=2)
        expanded = jnp.dot(
            pair_rows.reshape(-1, offset_count), selector, preferred_element_type=jnp.float32
        )
        coupling = expanded.astype(jnp.bfloat16).reshape(
            2, directions_here, target_block, source_count, box_count, box_count
        )
        values = source_block.reshape(directions_here, 2 * illum_here, source_count, box_count)
        combos = jnp.einsum(
            "klcy,qkacxy->klqax", values, coupling, preferred_element_type=jnp.float32
        )
        combos = combos.reshape(directions_here, 2, illum_here, 2, target_block * box_count)
        incoming_real = combos[:, 0, :, 0] - combos[:, 1, :, 1]
        incoming_imag = combos[:, 1, :, 0] + combos[:, 0, :, 1]
        return jnp.stack([incoming_real, incoming_imag], axis=1)

    slab_first = lax.axis_index("slab") * own_rows

    def block_rows(block_index):
        return translate(block_index * target_block, slab_first, outgoing)

    summed = lax.psum_scatter(
        lax.map(block_rows, jnp.arange(block_count * lax.axis_size("slab"), dtype=jnp.int32)),
        "slab",
        scatter_dimension=0,
        tiled=True,
    )
    incoming = summed.astype(jnp.bfloat16)
    incoming = incoming.reshape(incoming.shape[:4] + (target_block, box_count))
    item_rows = lax.all_to_all(incoming, "wide", split_axis=5, concat_axis=1, tiled=True)

    def product(left_side, right_side):
        return jnp.einsum(
            "bkrax,pk->baxrp", left_side, right_side, preferred_element_type=jnp.float32
        )

    items_real = item_rows[:, :, 0]
    items_imag = item_rows[:, :, 1]
    field_real = product(items_real, disaggregation[0]) - product(items_imag, disaggregation[1])
    field_imag = product(items_real, disaggregation[1]) + product(items_imag, disaggregation[0])
    stacked = jnp.stack([field_real, field_imag], axis=3).astype(jnp.bfloat16)
    return stacked.reshape((stacked.shape[0] * stacked.shape[1],) + stacked.shape[2:])


def local(wide, slab, sub, *args):
    source, aggregation, translators, _, _, box_offsets, _ = args
    rows, columns, _, illum, unknowns = source.shape
    share = aggregation.shape[1] // (wide * slab * sub)
    tiles = (
        2 * rows * columns == LANES
        and 2 * box_offsets.shape[0] == LANES
        and columns * wide == box_offsets.shape[0]
        and slab == 2
        and wide == 4
        and columns == 16
        and illum == 16
        and share % 32 == 0
        and unknowns == LANES
        and LANES < translators.shape[3] <= 2 * LANES
    )
    if tiles:
        return tiled_local(wide, slab, sub, *args)
    return general_local(*args)


def solution(mesh):
    placed = (
        P(("groups", "slab"), "wide", None, "sub", None),
        P(None, "groups", None),
        P(None, ("groups", "wide"), None, None),
        P(),
        P(),
        P(),
        P(None, None, "groups"),
    )
    return jax.shard_map(
        functools.partial(local, mesh.shape["wide"], mesh.shape["slab"], mesh.shape["sub"]),
        mesh=mesh,
        in_specs=placed,
        out_specs=P(("groups", "slab"), "wide", None, "sub", None),
        check_vma=False,
    )
```

```python
import functools

import jax
import jax.numpy as jnp
from jax import lax
from jax.experimental import pallas as pl
from jax.experimental.pallas import tpu as pltpu
from jax.sharding import PartitionSpec as P

OWNERS = ("wide", "slab", "sub")
LANES = 128
VMEM = 56 * 1024 * 1024
PITCH = 36
NT = (((1,), (1,)), ((), ()))
TN = (((0,), (0,)), ((), ()))


def outgoing_kernel(boxes, illum, devices, half, src_ref, agg_ref, out_ref, wide_src, wide_out):
    unknowns = src_ref.shape[1]
    wide_src[...] = src_ref[...].astype(jnp.float32)
    real = agg_ref[0].astype(jnp.float32)
    imag = agg_ref[1].astype(jnp.float32)

    def pick(array, part):
        return jnp.concatenate(
            [array[(2 * d + part) * half:(2 * d + part + 1) * half] for d in range(devices)], axis=0
        )

    real_low, real_high = pick(real, 0), pick(real, 1)
    imag_low, imag_high = pick(imag, 0), pick(imag, 1)
    to_real = jnp.concatenate([real_low, -imag_low, real_high, -imag_high], axis=1).astype(jnp.bfloat16)
    to_imag = jnp.concatenate([imag_low, real_low, imag_high, real_high], axis=1).astype(jnp.bfloat16)
    zeros = jnp.zeros((boxes, 2 * unknowns), jnp.bfloat16)
    rows = devices * half
    for r in range(illum):
        both = jnp.concatenate(
            [wide_src[pl.ds(q * illum + r, boxes, stride=2 * illum), :] for q in range(2)], axis=1
        ).astype(jnp.bfloat16)
        right = jnp.concatenate(
            [jnp.concatenate([both, zeros], axis=1), jnp.concatenate([zeros, both], axis=1)], axis=0
        )
        for q, left in ((0, to_real), (1, to_imag)):
            wide_out[pl.ds(q * illum + r, rows, stride=PITCH), :] = lax.dot_general(
                left, right, NT, preferred_element_type=jnp.float32
            )
    tall = 2 * illum
    for g in range(rows):
        out_ref[g * tall:(g + 1) * tall] = wide_out[g * PITCH:g * PITCH + tall].astype(jnp.bfloat16)


def expand_kernel(middle, base_ref, index_ref, table_ref, out_ref, choice, left, wide):
    batch, translators, offsets = table_ref.shape[1:]
    depth = out_ref.shape[3]
    tall = 2 * depth
    rows = 2 * batch * tall

    @pl.when(pl.program_id(0) == 0)
    def _():
        offset = lax.broadcasted_iota(jnp.int32, (2 * LANES, LANES), 0)
        for x in range(tall):
            choice[:, x * LANES:(x + 1) * LANES] = jnp.where(
                offset == index_ref[x:x + 1, :], 1.0, 0.0
            ).astype(jnp.bfloat16)
        left[...] = jnp.zeros_like(left)

    for q in range(2):
        for k in range(batch):
            row = (q * batch + k) * tall
            left[row:row + translators, 0:offsets] = table_ref[q, k]
    table = left[...]
    for x in range(0, tall, 2):
        picked = jnp.dot(
            table, choice[:, x * LANES:(x + 2) * LANES], preferred_element_type=jnp.float32
        )
        wide[pl.ds(x, rows, stride=PITCH), :] = picked[:, :LANES]
        wide[pl.ds(x + 1, rows, stride=PITCH), :] = picked[:, LANES:]
    for k in range(batch):
        for v in range(2):
            out_ref[v, k, middle] = jnp.zeros(out_ref.shape[3:], jnp.bfloat16)
        for t in range(translators):
            if abs(t - middle) < 2:
                continue
            for q in range(2):
                row = ((q * batch + k) * tall + t) * PITCH
                for v in range(2):
                    out_ref[v, k, t, :, q * LANES:(q + 1) * LANES] = wide[
                        row + v * depth:row + (v + 1) * depth
                    ].astype(jnp.bfloat16)


def translate_kernel(wide, slab, sub, rows, columns, pair_ref, src_ref, exp_ref, out_ref):
    illum = src_ref.shape[3]
    steps = exp_ref.shape[2]
    all_rows = slab * rows
    lane = lax.broadcasted_iota(jnp.int32, (illum, LANES), 1)
    group = lane // columns
    groups = LANES // columns
    lower = lane < LANES // 2
    zero = jnp.zeros((illum, LANES), jnp.bfloat16)
    for step in range(steps):
        here = pl.program_id(0) * steps + step
        sums = [None, None]
        turned = {}

        def turn(s, u, q, w, amount):
            key = (s, u, q, w, amount)
            if key not in turned:
                tile = src_ref[(w * slab + s) * sub + u, here, q]
                turned[key] = pltpu.roll(tile, amount * columns, 1) if amount else tile
            return turned[key]

        for c in range(all_rows):
            s, own = c // rows, c % rows
            for k2 in range(2):
                position = k2 * rows + own
                parts = {}
                for u in range(sub):
                    for q in range(2):
                        for h in range(2):
                            tile = zero
                            for w in range(wide):
                                place = h * wide + w
                                tile = jnp.where(
                                    group == place,
                                    turn(s, u, q, w, (place - position) % groups),
                                    tile,
                                )
                            parts[u, q, h] = tile
                left = []
                for h in range(2):
                    for u in range(sub):
                        left.append(jnp.concatenate([parts[u, 0, h], -parts[u, 1, h]], axis=1))
                        left.append(jnp.concatenate([parts[u, 1, h], parts[u, 0, h]], axis=1))
                left = jnp.concatenate(left, axis=0)
                right = jnp.concatenate(
                    [exp_ref[0, k2, step, pair_ref[a * all_rows + c]] for a in range(all_rows)], axis=0
                )
                product = lax.dot_general(left, right, NT, preferred_element_type=jnp.float32)
                sums[k2] = product if sums[k2] is None else sums[k2] + product
        for h in range(2):
            for u in range(sub):
                for q in range(2):
                    row = ((h * sub + u) * 2 + q) * illum
                    first = sums[0][row:row + illum]
                    second = sums[1][row:row + illum]
                    for s in range(slab):
                        if s == 0:
                            tile = jnp.where(lower, first, pltpu.roll(second, LANES // 2, 1))
                        else:
                            tile = jnp.where(lower, pltpu.roll(first, LANES // 2, 1), second)
                        out_ref[(h * slab + s) * sub + u, here, q] = tile.astype(jnp.bfloat16)


def pattern_kernel(devices, half, place_ref, dis_ref, out_ref):
    real = dis_ref[0].astype(jnp.float32).T
    imag = dis_ref[1].astype(jnp.float32).T

    def pick(array, part):
        return jnp.concatenate(
            [array[(2 * d + part) * half:(2 * d + part + 1) * half] for d in range(devices)], axis=0
        )

    sides = []
    for part in range(2):
        real_part, imag_part = pick(real, part), pick(imag, part)
        sides.append(
            jnp.concatenate(
                [
                    jnp.concatenate([real_part, imag_part], axis=1),
                    jnp.concatenate([-imag_part, real_part], axis=1),
                ],
                axis=0,
            )
        )
    out_ref[...] = jnp.concatenate(sides, axis=1).astype(jnp.bfloat16)


def field_kernel(boxes, illum, inc_ref, pattern_ref, out_ref, wide_inc, wide_out):
    unknowns = out_ref.shape[1]
    tall = 2 * illum
    rows = inc_ref.shape[0] // tall
    for g in range(rows):
        wide_inc[g * PITCH:g * PITCH + tall] = inc_ref[g * tall:(g + 1) * tall].astype(jnp.float32)
    right = pattern_ref[...]
    for r in range(illum):
        left = jnp.concatenate(
            [wide_inc[pl.ds(q * illum + r, rows, stride=PITCH), :] for q in range(2)], axis=0
        ).astype(jnp.bfloat16)
        product = lax.dot_general(left, right, TN, preferred_element_type=jnp.float32)
        total = product[:boxes, :2 * unknowns] + product[boxes:, 2 * unknowns:]
        for q in range(2):
            wide_out[pl.ds(q * illum + r, boxes, stride=PITCH), :] = total[
                :, q * unknowns:(q + 1) * unknowns
            ]
    for g in range(boxes):
        out_ref[g * tall:(g + 1) * tall] = wide_out[g * PITCH:g * PITCH + tall].astype(out_ref.dtype)


def tiled_local(wide, slab, sub, source, aggregation, translators, tile_map, far_mask, box_offsets, disaggregation):
    rows, columns, _, illum, unknowns = source.shape
    devices = wide * slab * sub
    directions = aggregation.shape[1]
    half = directions // devices // 2
    boxes = rows * columns
    all_rows = slab * rows
    count = translators.shape[2]
    offsets = translators.shape[3]
    middle = count // 2
    params = pltpu.CompilerParams(vmem_limit_bytes=VMEM)

    lines = devices * half * 2 * illum
    outgoing = pl.pallas_call(
        functools.partial(outgoing_kernel, boxes, illum, devices, half),
        out_shape=jax.ShapeDtypeStruct((lines, LANES), jnp.bfloat16),
        scratch_shapes=[
            pltpu.VMEM((boxes * 2 * illum, unknowns), jnp.float32),
            pltpu.VMEM((devices * half * PITCH, LANES), jnp.float32),
        ],
        compiler_params=params,
        name="outgoing",
    )(source.reshape(boxes * 2 * illum, unknowns), aggregation)
    block = (devices, half, 2, illum, LANES)
    received = lax.all_to_all(outgoing.reshape(block), OWNERS, split_axis=0, concat_axis=0, tiled=True)

    side = box_offsets.shape[0]
    x_half = side // 2
    place = lax.axis_index("wide") // 2
    by_side = jnp.where(place == 0, jnp.roll(box_offsets, x_half, axis=0), box_offsets)
    by_side = by_side.reshape(2, 2, columns, side)
    index = jnp.concatenate([by_side[:, 0], by_side[:, 1]], axis=-1).reshape(x_half, 2 * side)
    base = lax.axis_index("slab") * sub + lax.axis_index("sub")
    near = devices // 2
    pattern = pl.pallas_call(
        functools.partial(pattern_kernel, near, half),
        grid_spec=pltpu.PrefetchScalarGridSpec(
            num_scalar_prefetch=1,
            grid=(1,),
            in_specs=[pl.BlockSpec((2, unknowns, directions // 2), lambda i, place: (0, 0, place[0]))],
            out_specs=pl.BlockSpec((2 * near * half, 4 * unknowns), lambda i, place: (0, 0)),
        ),
        out_shape=jax.ShapeDtypeStruct((2 * near * half, 4 * unknowns), jnp.bfloat16),
        compiler_params=params,
        name="pattern",
    )(place.reshape(1), disaggregation)
    index, pattern = lax.optimization_barrier((index, pattern))
    batch = 4
    expanded = pl.pallas_call(
        functools.partial(expand_kernel, middle),
        grid_spec=pltpu.PrefetchScalarGridSpec(
            num_scalar_prefetch=1,
            grid=(2 * half // batch,),
            in_specs=[
                pl.BlockSpec((x_half, 2 * side), lambda k, base: (0, 0)),
                pl.BlockSpec(
                    (2, batch, count, offsets), lambda k, base: (0, base[0] * (2 * half // batch) + k, 0, 0)
                ),
            ],
            out_specs=pl.BlockSpec(
                (2, batch, count, columns, 2 * LANES), lambda k, base: (0, k, 0, 0, 0)
            ),
            scratch_shapes=[
                pltpu.VMEM((2 * LANES, x_half * LANES), jnp.bfloat16),
                pltpu.VMEM((2 * batch * x_half, 2 * LANES), jnp.bfloat16),
                pltpu.VMEM((2 * batch * x_half * PITCH, LANES), jnp.float32),
            ],
        ),
        out_shape=jax.ShapeDtypeStruct((2, 2 * half, count, columns, 2 * LANES), jnp.bfloat16),
        compiler_params=params,
        name="expand",
    )(base.reshape(1), index, translators)
    expanded = expanded.reshape(2, 2, half, count, columns, 2 * LANES)

    pairs = jnp.where(far_mask == 1, tile_map, middle).reshape(-1)
    lines = lines // 2
    shape = (boxes * 2 * illum, unknowns)
    neighbours = [[first * near + d for d in range(near)] for first in range(2)]
    steps = 4

    def translate(v):
        return pl.pallas_call(
            functools.partial(translate_kernel, wide, slab, sub, rows, columns),
            grid_spec=pltpu.PrefetchScalarGridSpec(
                num_scalar_prefetch=1,
                grid=(half // steps,),
                in_specs=[
                    pl.BlockSpec(block, lambda k, pairs: (0, 0, 0, 0, 0)),
                    pl.BlockSpec(
                        (1, 2, steps, count, columns, 2 * LANES), lambda k, pairs: (v, 0, k, 0, 0, 0)
                    ),
                ],
                out_specs=pl.BlockSpec((near,) + block[1:], lambda k, pairs: (0, 0, 0, 0, 0)),
            ),
            out_shape=jax.ShapeDtypeStruct((near,) + block[1:], jnp.bfloat16),
            compiler_params=params,
            name="translate",
        )(pairs, received, expanded)

    def exchange(values):
        return lax.all_to_all(
            values, OWNERS, split_axis=0, concat_axis=0, tiled=True, axis_index_groups=neighbours
        )

    def field(values, kind):
        return pl.pallas_call(
            functools.partial(field_kernel, boxes, illum),
            out_shape=jax.ShapeDtypeStruct(shape, kind),
            scratch_shapes=[
                pltpu.VMEM((near * half * PITCH, LANES), jnp.float32),
                pltpu.VMEM((boxes * PITCH, unknowns), jnp.float32),
            ],
            compiler_params=params,
            name="field",
        )(values.reshape(lines, LANES), pattern)

    far_half = exchange(translate(0))
    near_half = exchange(translate(1))
    across = lax.ppermute(
        field(far_half, jnp.bfloat16), "wide", [(w, (w + wide // 2) % wide) for w in range(wide)]
    )
    total = field(near_half, jnp.float32) + across.astype(jnp.float32)
    return total.astype(jnp.bfloat16).reshape(source.shape)


def aggregate(values, pattern_real, pattern_imag):

    def product(left_side, right_side):
        return jnp.einsum(
            "axrp,kp->krax", left_side, right_side, preferred_element_type=jnp.float32
        )

    values_real = values[:, :, 0]
    values_imag = values[:, :, 1]
    out_real = product(values_real, pattern_real) - product(values_imag, pattern_imag)
    out_imag = product(values_real, pattern_imag) + product(values_imag, pattern_real)
    return jnp.stack([out_real, out_imag], axis=1).astype(jnp.bfloat16)


def general_local(source, aggregation, translators, tile_map, far_mask, box_offsets, disaggregation):
    own_rows = source.shape[0]
    tile_count = translators.shape[2]
    offset_count = translators.shape[3]
    box_count = box_offsets.shape[0]
    target_block = 2
    block_count = own_rows // target_block
    outgoing = lax.all_to_all(
        aggregate(source, aggregation[0], aggregation[1]),
        "wide",
        split_axis=0,
        concat_axis=4,
        tiled=True,
    )
    directions_here = outgoing.shape[0]
    illum_here = outgoing.shape[2]
    row_table = jnp.concatenate(
        [translators, jnp.zeros((2, directions_here, 1, offset_count), jnp.bfloat16)], axis=2
    )
    offset_ids = lax.broadcasted_iota(jnp.int32, (offset_count, box_count, box_count), 0)
    selector = (offset_ids == box_offsets[None, :, :]).astype(jnp.bfloat16)
    selector = selector.reshape(offset_count, box_count * box_count)

    def translate(target_first, source_first, source_block):
        source_count = source_block.shape[3]
        pair_map = lax.dynamic_slice(
            tile_map, (target_first, source_first), (target_block, source_count)
        )
        pair_far = lax.dynamic_slice(
            far_mask, (target_first, source_first), (target_block, source_count)
        )
        pair_index = jnp.where(pair_far == 1, pair_map, tile_count)
        pair_rows = jnp.take(row_table, pair_index.reshape(-1), axis=2)
        expanded = jnp.dot(
            pair_rows.reshape(-1, offset_count), selector, preferred_element_type=jnp.float32
        )
        coupling = expanded.astype(jnp.bfloat16).reshape(
            2, directions_here, target_block, source_count, box_count, box_count
        )
        values = source_block.reshape(directions_here, 2 * illum_here, source_count, box_count)
        combos = jnp.einsum(
            "klcy,qkacxy->klqax", values, coupling, preferred_element_type=jnp.float32
        )
        combos = combos.reshape(directions_here, 2, illum_here, 2, target_block * box_count)
        incoming_real = combos[:, 0, :, 0] - combos[:, 1, :, 1]
        incoming_imag = combos[:, 1, :, 0] + combos[:, 0, :, 1]
        return jnp.stack([incoming_real, incoming_imag], axis=1)

    slab_first = lax.axis_index("slab") * own_rows

    def block_rows(block_index):
        return translate(block_index * target_block, slab_first, outgoing)

    summed = lax.psum_scatter(
        lax.map(block_rows, jnp.arange(block_count * lax.axis_size("slab"), dtype=jnp.int32)),
        "slab",
        scatter_dimension=0,
        tiled=True,
    )
    incoming = summed.astype(jnp.bfloat16)
    incoming = incoming.reshape(incoming.shape[:4] + (target_block, box_count))
    item_rows = lax.all_to_all(incoming, "wide", split_axis=5, concat_axis=1, tiled=True)

    def product(left_side, right_side):
        return jnp.einsum(
            "bkrax,pk->baxrp", left_side, right_side, preferred_element_type=jnp.float32
        )

    items_real = item_rows[:, :, 0]
    items_imag = item_rows[:, :, 1]
    field_real = product(items_real, disaggregation[0]) - product(items_imag, disaggregation[1])
    field_imag = product(items_real, disaggregation[1]) + product(items_imag, disaggregation[0])
    stacked = jnp.stack([field_real, field_imag], axis=3).astype(jnp.bfloat16)
    return stacked.reshape((stacked.shape[0] * stacked.shape[1],) + stacked.shape[2:])


def local(wide, slab, sub, *args):
    source, aggregation, translators, _, _, box_offsets, _ = args
    rows, columns, _, illum, unknowns = source.shape
    share = aggregation.shape[1] // (wide * slab * sub)
    tiles = (
        2 * rows * columns == LANES
        and 2 * box_offsets.shape[0] == LANES
        and columns * wide == box_offsets.shape[0]
        and slab == 2
        and wide == 4
        and columns == 16
        and illum == 16
        and share % 32 == 0
        and unknowns == LANES
        and LANES < translators.shape[3] <= 2 * LANES
        and translators.shape[2] <= 32
    )
    if tiles:
        return tiled_local(wide, slab, sub, *args)
    return general_local(*args)


def solution(mesh):
    placed = (
        P(("groups", "slab"), "wide", None, "sub", None),
        P(None, "groups", None),
        P(None, ("groups", "wide"), None, None),
        P(),
        P(),
        P(),
        P(None, None, "groups"),
    )
    return jax.shard_map(
        functools.partial(local, mesh.shape["wide"], mesh.shape["slab"], mesh.shape["sub"]),
        mesh=mesh,
        in_specs=placed,
        out_specs=P(("groups", "slab"), "wide", None, "sub", None),
        check_vma=False,
    )
```

```python
import functools

import jax
import jax.numpy as jnp
from jax import lax
from jax.experimental import pallas as pl
from jax.experimental.pallas import tpu as pltpu
from jax.sharding import PartitionSpec as P

OWNERS = ("wide", "slab", "sub")
LANES = 128
MIB = 1024 * 1024
PITCH = 36
NT = (((1,), (1,)), ((), ()))
TN = (((0,), (0,)), ((), ()))


def outgoing_kernel(boxes, illum, devices, half, src_ref, agg_ref, out_ref, wide_src, wide_out):
    unknowns = src_ref.shape[1]
    wide_src[...] = src_ref[...].astype(jnp.float32)
    real = agg_ref[0].astype(jnp.float32)
    imag = agg_ref[1].astype(jnp.float32)

    def pick(array, part):
        return jnp.concatenate(
            [array[(2 * d + part) * half:(2 * d + part + 1) * half] for d in range(devices)], axis=0
        )

    real_low, real_high = pick(real, 0), pick(real, 1)
    imag_low, imag_high = pick(imag, 0), pick(imag, 1)
    to_real = jnp.concatenate([real_low, -imag_low, real_high, -imag_high], axis=1).astype(jnp.bfloat16)
    to_imag = jnp.concatenate([imag_low, real_low, imag_high, real_high], axis=1).astype(jnp.bfloat16)
    zeros = jnp.zeros((boxes, 2 * unknowns), jnp.bfloat16)
    rows = devices * half
    for r in range(illum):
        both = jnp.concatenate(
            [wide_src[pl.ds(q * illum + r, boxes, stride=2 * illum), :] for q in range(2)], axis=1
        ).astype(jnp.bfloat16)
        right = jnp.concatenate(
            [jnp.concatenate([both, zeros], axis=1), jnp.concatenate([zeros, both], axis=1)], axis=0
        )
        for q, left in ((0, to_real), (1, to_imag)):
            wide_out[pl.ds(q * illum + r, rows, stride=PITCH), :] = lax.dot_general(
                left, right, NT, preferred_element_type=jnp.float32
            )
    tall = 2 * illum
    for g in range(rows):
        out_ref[g * tall:(g + 1) * tall] = wide_out[g * PITCH:g * PITCH + tall].astype(jnp.bfloat16)


def expand_kernel(middle, base_ref, index_ref, table_ref, out_ref, choice, left, wide):
    batch, translators, offsets = table_ref.shape[1:]
    depth = out_ref.shape[3]
    tall = 2 * depth
    rows = 2 * batch * tall

    @pl.when(pl.program_id(0) == 0)
    def _():
        offset = lax.broadcasted_iota(jnp.int32, (2 * LANES, LANES), 0)
        for x in range(tall):
            choice[:, x * LANES:(x + 1) * LANES] = jnp.where(
                offset == index_ref[x:x + 1, :], 1.0, 0.0
            ).astype(jnp.bfloat16)
        left[...] = jnp.zeros_like(left)

    for q in range(2):
        for k in range(batch):
            row = (q * batch + k) * tall
            left[row:row + translators, 0:offsets] = table_ref[q, k]
    table = left[...]
    for x in range(0, tall, 2):
        picked = jnp.dot(
            table, choice[:, x * LANES:(x + 2) * LANES], preferred_element_type=jnp.float32
        )
        wide[pl.ds(x, rows, stride=PITCH), :] = picked[:, :LANES]
        wide[pl.ds(x + 1, rows, stride=PITCH), :] = picked[:, LANES:]
    for k in range(batch):
        for v in range(2):
            out_ref[v, k, middle] = jnp.zeros(out_ref.shape[3:], jnp.bfloat16)
        for t in range(translators):
            if abs(t - middle) < 2:
                continue
            for q in range(2):
                row = ((q * batch + k) * tall + t) * PITCH
                for v in range(2):
                    out_ref[v, k, t, :, q * LANES:(q + 1) * LANES] = wide[
                        row + v * depth:row + (v + 1) * depth
                    ].astype(jnp.bfloat16)


def translate_kernel(wide, slab, sub, rows, columns, pair_ref, src_ref, exp_ref, out_ref):
    illum = src_ref.shape[3]
    steps = exp_ref.shape[2]
    all_rows = slab * rows
    lane = lax.broadcasted_iota(jnp.int32, (illum, LANES), 1)
    group = lane // columns
    groups = LANES // columns
    lower = lane < LANES // 2
    zero = jnp.zeros((illum, LANES), jnp.bfloat16)
    for step in range(steps):
        here = pl.program_id(0) * steps + step
        sums = [None, None]
        turned = {}

        def turn(s, u, q, w, amount):
            key = (s, u, q, w, amount)
            if key not in turned:
                tile = src_ref[(w * slab + s) * sub + u, here, q]
                turned[key] = pltpu.roll(tile, amount * columns, 1) if amount else tile
            return turned[key]

        for c in range(all_rows):
            s, own = c // rows, c % rows
            for k2 in range(2):
                position = k2 * rows + own
                parts = {}
                for u in range(sub):
                    for q in range(2):
                        for h in range(2):
                            tile = zero
                            for w in range(wide):
                                place = h * wide + w
                                tile = jnp.where(
                                    group == place,
                                    turn(s, u, q, w, (place - position) % groups),
                                    tile,
                                )
                            parts[u, q, h] = tile
                left = []
                for h in range(2):
                    for u in range(sub):
                        left.append(jnp.concatenate([parts[u, 0, h], -parts[u, 1, h]], axis=1))
                        left.append(jnp.concatenate([parts[u, 1, h], parts[u, 0, h]], axis=1))
                left = jnp.concatenate(left, axis=0)
                right = jnp.concatenate(
                    [exp_ref[0, k2, step, pair_ref[a * all_rows + c]] for a in range(all_rows)], axis=0
                )
                product = lax.dot_general(left, right, NT, preferred_element_type=jnp.float32)
                sums[k2] = product if sums[k2] is None else sums[k2] + product
        for h in range(2):
            for u in range(sub):
                for q in range(2):
                    row = ((h * sub + u) * 2 + q) * illum
                    first = sums[0][row:row + illum]
                    second = sums[1][row:row + illum]
                    for s in range(slab):
                        if s == 0:
                            tile = jnp.where(lower, first, pltpu.roll(second, LANES // 2, 1))
                        else:
                            tile = jnp.where(lower, pltpu.roll(first, LANES // 2, 1), second)
                        out_ref[(h * slab + s) * sub + u, here, q] = tile.astype(jnp.bfloat16)


def pattern_kernel(devices, half, place_ref, dis_ref, out_ref):
    real = dis_ref[0].astype(jnp.float32).T
    imag = dis_ref[1].astype(jnp.float32).T

    def pick(array, part):
        return jnp.concatenate(
            [array[(2 * d + part) * half:(2 * d + part + 1) * half] for d in range(devices)], axis=0
        )

    sides = []
    for part in range(2):
        real_part, imag_part = pick(real, part), pick(imag, part)
        sides.append(
            jnp.concatenate(
                [
                    jnp.concatenate([real_part, imag_part], axis=1),
                    jnp.concatenate([-imag_part, real_part], axis=1),
                ],
                axis=0,
            )
        )
    out_ref[...] = jnp.concatenate(sides, axis=1).astype(jnp.bfloat16)


def field_kernel(boxes, illum, inc_ref, pattern_ref, out_ref, wide_inc, wide_out):
    unknowns = out_ref.shape[1]
    tall = 2 * illum
    rows = inc_ref.shape[0] // tall
    for g in range(rows):
        wide_inc[g * PITCH:g * PITCH + tall] = inc_ref[g * tall:(g + 1) * tall].astype(jnp.float32)
    right = pattern_ref[...]
    for r in range(illum):
        left = jnp.concatenate(
            [wide_inc[pl.ds(q * illum + r, rows, stride=PITCH), :] for q in range(2)], axis=0
        ).astype(jnp.bfloat16)
        product = lax.dot_general(left, right, TN, preferred_element_type=jnp.float32)
        total = product[:boxes, :2 * unknowns] + product[boxes:, 2 * unknowns:]
        for q in range(2):
            wide_out[pl.ds(q * illum + r, boxes, stride=PITCH), :] = total[
                :, q * unknowns:(q + 1) * unknowns
            ]
    for g in range(boxes):
        out_ref[g * tall:(g + 1) * tall] = wide_out[g * PITCH:g * PITCH + tall].astype(out_ref.dtype)


def tiled_local(wide, slab, sub, source, aggregation, translators, tile_map, far_mask, box_offsets, disaggregation):
    rows, columns, _, illum, unknowns = source.shape
    devices = wide * slab * sub
    directions = aggregation.shape[1]
    half = directions // devices // 2
    boxes = rows * columns
    all_rows = slab * rows
    count = translators.shape[2]
    offsets = translators.shape[3]
    middle = count // 2

    lines = devices * half * 2 * illum
    outgoing = pl.pallas_call(
        functools.partial(outgoing_kernel, boxes, illum, devices, half),
        out_shape=jax.ShapeDtypeStruct((lines, LANES), jnp.bfloat16),
        scratch_shapes=[
            pltpu.VMEM((boxes * 2 * illum, unknowns), jnp.float32),
            pltpu.VMEM((devices * half * PITCH, LANES), jnp.float32),
        ],
        compiler_params=pltpu.CompilerParams(vmem_limit_bytes=56 * MIB),
        name="outgoing",
    )(source.reshape(boxes * 2 * illum, unknowns), aggregation)
    block = (devices, half, 2, illum, LANES)
    received = lax.all_to_all(outgoing.reshape(block), OWNERS, split_axis=0, concat_axis=0, tiled=True)

    side = box_offsets.shape[0]
    x_half = side // 2
    place = lax.axis_index("wide") // 2
    by_side = jnp.where(place == 0, jnp.roll(box_offsets, x_half, axis=0), box_offsets)
    by_side = by_side.reshape(2, 2, columns, side)
    index = jnp.concatenate([by_side[:, 0], by_side[:, 1]], axis=-1).reshape(x_half, 2 * side)
    base = lax.axis_index("slab") * sub + lax.axis_index("sub")
    near = devices // 2
    pattern = pl.pallas_call(
        functools.partial(pattern_kernel, near, half),
        grid_spec=pltpu.PrefetchScalarGridSpec(
            num_scalar_prefetch=1,
            grid=(1,),
            in_specs=[pl.BlockSpec((2, unknowns, directions // 2), lambda i, place: (0, 0, place[0]))],
            out_specs=pl.BlockSpec((2 * near * half, 4 * unknowns), lambda i, place: (0, 0)),
        ),
        out_shape=jax.ShapeDtypeStruct((2 * near * half, 4 * unknowns), jnp.bfloat16),
        compiler_params=pltpu.CompilerParams(vmem_limit_bytes=8 * MIB),
        name="pattern",
    )(place.reshape(1), disaggregation)
    index, pattern = lax.optimization_barrier((index, pattern))
    batch = 4
    expanded = pl.pallas_call(
        functools.partial(expand_kernel, middle),
        grid_spec=pltpu.PrefetchScalarGridSpec(
            num_scalar_prefetch=1,
            grid=(2 * half // batch,),
            in_specs=[
                pl.BlockSpec((x_half, 2 * side), lambda k, base: (0, 0)),
                pl.BlockSpec(
                    (2, batch, count, offsets), lambda k, base: (0, base[0] * (2 * half // batch) + k, 0, 0)
                ),
            ],
            out_specs=pl.BlockSpec(
                (2, batch, count, columns, 2 * LANES), lambda k, base: (0, k, 0, 0, 0)
            ),
            scratch_shapes=[
                pltpu.VMEM((2 * LANES, x_half * LANES), jnp.bfloat16),
                pltpu.VMEM((2 * batch * x_half, 2 * LANES), jnp.bfloat16),
                pltpu.VMEM((2 * batch * x_half * PITCH, LANES), jnp.float32),
            ],
        ),
        out_shape=jax.ShapeDtypeStruct((2, 2 * half, count, columns, 2 * LANES), jnp.bfloat16),
        compiler_params=pltpu.CompilerParams(vmem_limit_bytes=56 * MIB),
        name="expand",
    )(base.reshape(1), index, translators)
    expanded = expanded.reshape(2, 2, half, count, columns, 2 * LANES)

    pairs = jnp.where(far_mask == 1, tile_map, middle).reshape(-1)
    lines = lines // 2
    shape = (boxes * 2 * illum, unknowns)
    neighbours = [[first * near + d for d in range(near)] for first in range(2)]
    steps = 4

    def translate(v):
        return pl.pallas_call(
            functools.partial(translate_kernel, wide, slab, sub, rows, columns),
            grid_spec=pltpu.PrefetchScalarGridSpec(
                num_scalar_prefetch=1,
                grid=(half // steps,),
                in_specs=[
                    pl.BlockSpec(block, lambda k, pairs: (0, 0, 0, 0, 0)),
                    pl.BlockSpec(
                        (1, 2, steps, count, columns, 2 * LANES), lambda k, pairs: (v, 0, k, 0, 0, 0)
                    ),
                ],
                out_specs=pl.BlockSpec((near,) + block[1:], lambda k, pairs: (0, 0, 0, 0, 0)),
            ),
            out_shape=jax.ShapeDtypeStruct((near,) + block[1:], jnp.bfloat16),
            compiler_params=pltpu.CompilerParams(vmem_limit_bytes=50 * MIB),
            name="translate",
        )(pairs, received, expanded)

    def exchange(values):
        return lax.all_to_all(
            values, OWNERS, split_axis=0, concat_axis=0, tiled=True, axis_index_groups=neighbours
        )

    def field(values, kind):
        return pl.pallas_call(
            functools.partial(field_kernel, boxes, illum),
            out_shape=jax.ShapeDtypeStruct(shape, kind),
            scratch_shapes=[
                pltpu.VMEM((near * half * PITCH, LANES), jnp.float32),
                pltpu.VMEM((boxes * PITCH, unknowns), jnp.float32),
            ],
            compiler_params=pltpu.CompilerParams(vmem_limit_bytes=12 * MIB),
            name="field",
        )(values.reshape(lines, LANES), pattern)

    far_half = exchange(translate(0))
    near_half = exchange(translate(1))
    across = lax.ppermute(
        field(far_half, jnp.bfloat16), "wide", [(w, (w + wide // 2) % wide) for w in range(wide)]
    )
    total = field(near_half, jnp.float32) + across.astype(jnp.float32)
    return total.astype(jnp.bfloat16).reshape(source.shape)


def aggregate(values, pattern_real, pattern_imag):

    def product(left_side, right_side):
        return jnp.einsum(
            "axrp,kp->krax", left_side, right_side, preferred_element_type=jnp.float32
        )

    values_real = values[:, :, 0]
    values_imag = values[:, :, 1]
    out_real = product(values_real, pattern_real) - product(values_imag, pattern_imag)
    out_imag = product(values_real, pattern_imag) + product(values_imag, pattern_real)
    return jnp.stack([out_real, out_imag], axis=1).astype(jnp.bfloat16)


def general_local(source, aggregation, translators, tile_map, far_mask, box_offsets, disaggregation):
    own_rows = source.shape[0]
    tile_count = translators.shape[2]
    offset_count = translators.shape[3]
    box_count = box_offsets.shape[0]
    target_block = 2
    block_count = own_rows // target_block
    outgoing = lax.all_to_all(
        aggregate(source, aggregation[0], aggregation[1]),
        "wide",
        split_axis=0,
        concat_axis=4,
        tiled=True,
    )
    directions_here = outgoing.shape[0]
    illum_here = outgoing.shape[2]
    row_table = jnp.concatenate(
        [translators, jnp.zeros((2, directions_here, 1, offset_count), jnp.bfloat16)], axis=2
    )
    offset_ids = lax.broadcasted_iota(jnp.int32, (offset_count, box_count, box_count), 0)
    selector = (offset_ids == box_offsets[None, :, :]).astype(jnp.bfloat16)
    selector = selector.reshape(offset_count, box_count * box_count)

    def translate(target_first, source_first, source_block):
        source_count = source_block.shape[3]
        pair_map = lax.dynamic_slice(
            tile_map, (target_first, source_first), (target_block, source_count)
        )
        pair_far = lax.dynamic_slice(
            far_mask, (target_first, source_first), (target_block, source_count)
        )
        pair_index = jnp.where(pair_far == 1, pair_map, tile_count)
        pair_rows = jnp.take(row_table, pair_index.reshape(-1), axis=2)
        expanded = jnp.dot(
            pair_rows.reshape(-1, offset_count), selector, preferred_element_type=jnp.float32
        )
        coupling = expanded.astype(jnp.bfloat16).reshape(
            2, directions_here, target_block, source_count, box_count, box_count
        )
        values = source_block.reshape(directions_here, 2 * illum_here, source_count, box_count)
        combos = jnp.einsum(
            "klcy,qkacxy->klqax", values, coupling, preferred_element_type=jnp.float32
        )
        combos = combos.reshape(directions_here, 2, illum_here, 2, target_block * box_count)
        incoming_real = combos[:, 0, :, 0] - combos[:, 1, :, 1]
        incoming_imag = combos[:, 1, :, 0] + combos[:, 0, :, 1]
        return jnp.stack([incoming_real, incoming_imag], axis=1)

    slab_first = lax.axis_index("slab") * own_rows

    def block_rows(block_index):
        return translate(block_index * target_block, slab_first, outgoing)

    summed = lax.psum_scatter(
        lax.map(block_rows, jnp.arange(block_count * lax.axis_size("slab"), dtype=jnp.int32)),
        "slab",
        scatter_dimension=0,
        tiled=True,
    )
    incoming = summed.astype(jnp.bfloat16)
    incoming = incoming.reshape(incoming.shape[:4] + (target_block, box_count))
    item_rows = lax.all_to_all(incoming, "wide", split_axis=5, concat_axis=1, tiled=True)

    def product(left_side, right_side):
        return jnp.einsum(
            "bkrax,pk->baxrp", left_side, right_side, preferred_element_type=jnp.float32
        )

    items_real = item_rows[:, :, 0]
    items_imag = item_rows[:, :, 1]
    field_real = product(items_real, disaggregation[0]) - product(items_imag, disaggregation[1])
    field_imag = product(items_real, disaggregation[1]) + product(items_imag, disaggregation[0])
    stacked = jnp.stack([field_real, field_imag], axis=3).astype(jnp.bfloat16)
    return stacked.reshape((stacked.shape[0] * stacked.shape[1],) + stacked.shape[2:])


def local(wide, slab, sub, *args):
    source, aggregation, translators, _, _, box_offsets, _ = args
    rows, columns, _, illum, unknowns = source.shape
    share = aggregation.shape[1] // (wide * slab * sub)
    tiles = (
        2 * rows * columns == LANES
        and 2 * box_offsets.shape[0] == LANES
        and columns * wide == box_offsets.shape[0]
        and slab == 2
        and wide == 4
        and columns == 16
        and illum == 16
        and share % 32 == 0
        and unknowns == LANES
        and LANES < translators.shape[3] <= 2 * LANES
        and translators.shape[2] <= 32
    )
    if tiles:
        return tiled_local(wide, slab, sub, *args)
    return general_local(*args)


def solution(mesh):
    placed = (
        P(("groups", "slab"), "wide", None, "sub", None),
        P(None, "groups", None),
        P(None, ("groups", "wide"), None, None),
        P(),
        P(),
        P(),
        P(None, None, "groups"),
    )
    return jax.shard_map(
        functools.partial(local, mesh.shape["wide"], mesh.shape["slab"], mesh.shape["sub"]),
        mesh=mesh,
        in_specs=placed,
        out_specs=P(("groups", "slab"), "wide", None, "sub", None),
        check_vma=False,
    )
```

```python
import functools

import jax
import jax.numpy as jnp
from jax import lax
from jax.experimental import pallas as pl
from jax.experimental.pallas import tpu as pltpu
from jax.sharding import PartitionSpec as P

OWNERS = ("wide", "slab", "sub")
LANES = 128
MIB = 1024 * 1024
PITCH = 36
NT = (((1,), (1,)), ((), ()))
TN = (((0,), (0,)), ((), ()))


def outgoing_kernel(boxes, illum, devices, half, place_ref, src_ref, agg_ref, out_ref, wide_src, wide_out):
    unknowns = src_ref.shape[1]
    wide_src[...] = src_ref[...].astype(jnp.float32)
    real = agg_ref[0].astype(jnp.float32)
    imag = agg_ref[1].astype(jnp.float32)

    def pick(array, part):
        return jnp.concatenate(
            [array[(2 * d + part) * half:(2 * d + part + 1) * half] for d in range(devices)], axis=0
        )

    real_low, real_high = pick(real, 0), pick(real, 1)
    imag_low, imag_high = pick(imag, 0), pick(imag, 1)
    to_real = jnp.concatenate([real_low, -imag_low, real_high, -imag_high], axis=1).astype(jnp.bfloat16)
    to_imag = jnp.concatenate([imag_low, real_low, imag_high, real_high], axis=1).astype(jnp.bfloat16)
    zeros = jnp.zeros((boxes, 2 * unknowns), jnp.bfloat16)
    rows = devices * half
    for r in range(illum):
        both = jnp.concatenate(
            [wide_src[pl.ds(q * illum + r, boxes, stride=2 * illum), :] for q in range(2)], axis=1
        ).astype(jnp.bfloat16)
        right = jnp.concatenate(
            [jnp.concatenate([both, zeros], axis=1), jnp.concatenate([zeros, both], axis=1)], axis=0
        )
        for q, left in ((0, to_real), (1, to_imag)):
            wide_out[pl.ds(q * illum + r, rows, stride=PITCH), :] = lax.dot_general(
                left, right, NT, preferred_element_type=jnp.float32
            )
    tall = 2 * illum
    for g in range(rows):
        out_ref[g * tall:(g + 1) * tall] = wide_out[g * PITCH:g * PITCH + tall].astype(jnp.bfloat16)


def expand_kernel(middle, base_ref, index_ref, table_ref, out_ref, choice, left, wide):
    batch, translators, offsets = table_ref.shape[1:]
    depth = out_ref.shape[3]
    tall = 2 * depth
    rows = 2 * batch * tall

    @pl.when(pl.program_id(0) == 0)
    def _():
        offset = lax.broadcasted_iota(jnp.int32, (2 * LANES, LANES), 0)
        for x in range(tall):
            choice[:, x * LANES:(x + 1) * LANES] = jnp.where(
                offset == index_ref[x:x + 1, :], 1.0, 0.0
            ).astype(jnp.bfloat16)
        left[...] = jnp.zeros_like(left)

    for q in range(2):
        for k in range(batch):
            row = (q * batch + k) * tall
            left[row:row + translators, 0:offsets] = table_ref[q, k]
    table = left[...]
    for x in range(0, tall, 2):
        picked = jnp.dot(
            table, choice[:, x * LANES:(x + 2) * LANES], preferred_element_type=jnp.float32
        )
        wide[pl.ds(x, rows, stride=PITCH), :] = picked[:, :LANES]
        wide[pl.ds(x + 1, rows, stride=PITCH), :] = picked[:, LANES:]
    for k in range(batch):
        for v in range(2):
            out_ref[v, k, middle] = jnp.zeros(out_ref.shape[3:], jnp.bfloat16)
        for t in range(translators):
            if abs(t - middle) < 2:
                continue
            for q in range(2):
                row = ((q * batch + k) * tall + t) * PITCH
                for v in range(2):
                    out_ref[v, k, t, :, q * LANES:(q + 1) * LANES] = wide[
                        row + v * depth:row + (v + 1) * depth
                    ].astype(jnp.bfloat16)


def translate_kernel(wide, slab, sub, rows, columns, pair_ref, own_ref, far_ref, low_ref, high_ref, out_ref):
    illum = own_ref.shape[3]
    steps = low_ref.shape[1]
    all_rows = slab * rows
    lane = lax.broadcasted_iota(jnp.int32, (illum, LANES), 1)
    group = lane // columns
    groups = LANES // columns
    lower = lane < LANES // 2
    zero = jnp.zeros((illum, LANES), jnp.bfloat16)
    for step in range(steps):
        here = pl.program_id(0) * steps + step
        sums = [None, None]
        turned = {}

        def turn(s, u, q, w, amount):
            key = (s, u, q, w, amount)
            if key not in turned:
                tile = (own_ref, far_ref)[w // 2][(w % 2 * slab + s) * sub + u, here, q]
                turned[key] = pltpu.roll(tile, amount * columns, 1) if amount else tile
            return turned[key]

        for c in range(all_rows):
            s, own = c // rows, c % rows
            for k2 in range(2):
                position = k2 * rows + own
                parts = {}
                for u in range(sub):
                    for q in range(2):
                        for h in range(2):
                            tile = zero
                            for w in range(wide):
                                place = h * wide + w
                                tile = jnp.where(
                                    group == place,
                                    turn(s, u, q, w, (place - position) % groups),
                                    tile,
                                )
                            parts[u, q, h] = tile
                left = []
                for h in range(2):
                    for u in range(sub):
                        left.append(jnp.concatenate([parts[u, 0, h], -parts[u, 1, h]], axis=1))
                        left.append(jnp.concatenate([parts[u, 1, h], parts[u, 0, h]], axis=1))
                left = jnp.concatenate(left, axis=0)
                right = jnp.concatenate(
                    [
                        (low_ref, high_ref)[k2][0, step, pair_ref[a * all_rows + c]]
                        for a in range(all_rows)
                    ],
                    axis=0,
                )
                product = lax.dot_general(left, right, NT, preferred_element_type=jnp.float32)
                sums[k2] = product if sums[k2] is None else sums[k2] + product
        for h in range(2):
            for u in range(sub):
                for q in range(2):
                    row = ((h * sub + u) * 2 + q) * illum
                    first = sums[0][row:row + illum]
                    second = sums[1][row:row + illum]
                    for s in range(slab):
                        if s == 0:
                            tile = jnp.where(lower, first, pltpu.roll(second, LANES // 2, 1))
                        else:
                            tile = jnp.where(lower, pltpu.roll(first, LANES // 2, 1), second)
                        out_ref[(h * slab + s) * sub + u, here, q] = tile.astype(jnp.bfloat16)


def pattern_kernel(devices, half, place_ref, dis_ref, out_ref):
    real = dis_ref[0].astype(jnp.float32).T
    imag = dis_ref[1].astype(jnp.float32).T

    def pick(array, part):
        return jnp.concatenate(
            [array[(2 * d + part) * half:(2 * d + part + 1) * half] for d in range(devices)], axis=0
        )

    sides = []
    for part in range(2):
        real_part, imag_part = pick(real, part), pick(imag, part)
        sides.append(
            jnp.concatenate(
                [
                    jnp.concatenate([real_part, imag_part], axis=1),
                    jnp.concatenate([-imag_part, real_part], axis=1),
                ],
                axis=0,
            )
        )
    out_ref[...] = jnp.concatenate(sides, axis=1).astype(jnp.bfloat16)


def field_kernel(boxes, illum, inc_ref, pattern_ref, out_ref, wide_inc, wide_out):
    unknowns = out_ref.shape[1]
    tall = 2 * illum
    rows = inc_ref.shape[0] // tall
    for g in range(rows):
        wide_inc[g * PITCH:g * PITCH + tall] = inc_ref[g * tall:(g + 1) * tall].astype(jnp.float32)
    right = pattern_ref[...]
    for r in range(illum):
        left = jnp.concatenate(
            [wide_inc[pl.ds(q * illum + r, rows, stride=PITCH), :] for q in range(2)], axis=0
        ).astype(jnp.bfloat16)
        product = lax.dot_general(left, right, TN, preferred_element_type=jnp.float32)
        total = product[:boxes, :2 * unknowns] + product[boxes:, 2 * unknowns:]
        for q in range(2):
            wide_out[pl.ds(q * illum + r, boxes, stride=PITCH), :] = total[
                :, q * unknowns:(q + 1) * unknowns
            ]
    for g in range(boxes):
        out_ref[g * tall:(g + 1) * tall] = wide_out[g * PITCH:g * PITCH + tall].astype(out_ref.dtype)


def tiled_local(wide, slab, sub, source, aggregation, translators, tile_map, far_mask, box_offsets, disaggregation):
    rows, columns, _, illum, unknowns = source.shape
    devices = wide * slab * sub
    directions = aggregation.shape[1]
    half = directions // devices // 2
    boxes = rows * columns
    all_rows = slab * rows
    count = translators.shape[2]
    offsets = translators.shape[3]
    middle = count // 2

    near = devices // 2
    lines = near * half * 2 * illum
    block = (near, half, 2, illum, LANES)
    shape = (boxes * 2 * illum, unknowns)
    place = lax.axis_index("wide") // 2
    neighbours = [[first * near + d for d in range(near)] for first in range(2)]

    def exchange(values):
        return lax.all_to_all(
            values, OWNERS, split_axis=0, concat_axis=0, tiled=True, axis_index_groups=neighbours
        )

    def cross(values):
        return lax.ppermute(values, "wide", [(w, (w + wide // 2) % wide) for w in range(wide)])

    def outgoing(values):
        return pl.pallas_call(
            functools.partial(outgoing_kernel, boxes, illum, near, half),
            grid_spec=pltpu.PrefetchScalarGridSpec(
                num_scalar_prefetch=1,
                grid=(1,),
                in_specs=[
                    pl.BlockSpec(shape, lambda i, place: (0, 0)),
                    pl.BlockSpec((2, directions // 2, unknowns), lambda i, place: (0, place[0], 0)),
                ],
                out_specs=pl.BlockSpec((lines, LANES), lambda i, place: (0, 0)),
                scratch_shapes=[
                    pltpu.VMEM(shape, jnp.float32),
                    pltpu.VMEM((near * half * PITCH, LANES), jnp.float32),
                ],
            ),
            out_shape=jax.ShapeDtypeStruct((lines, LANES), jnp.bfloat16),
            compiler_params=pltpu.CompilerParams(vmem_limit_bytes=56 * MIB),
            name="outgoing",
        )(place.reshape(1), values, aggregation).reshape(block)

    flat = source.reshape(shape)
    across_source = cross(flat)
    own = exchange(outgoing(flat))

    side = box_offsets.shape[0]
    x_half = side // 2
    by_side = jnp.roll(box_offsets, x_half, axis=0)
    by_side = jnp.where(place == 0, by_side, jnp.roll(box_offsets, x_half, axis=1))
    by_side = by_side.reshape(2, 2, columns, side)
    index = jnp.concatenate([by_side[:, 0], by_side[:, 1]], axis=-1).reshape(x_half, 2 * side)
    base = lax.axis_index("slab") * sub + lax.axis_index("sub")
    pattern = pl.pallas_call(
        functools.partial(pattern_kernel, near, half),
        grid_spec=pltpu.PrefetchScalarGridSpec(
            num_scalar_prefetch=1,
            grid=(1,),
            in_specs=[pl.BlockSpec((2, unknowns, directions // 2), lambda i, place: (0, 0, place[0]))],
            out_specs=pl.BlockSpec((2 * near * half, 4 * unknowns), lambda i, place: (0, 0)),
        ),
        out_shape=jax.ShapeDtypeStruct((2 * near * half, 4 * unknowns), jnp.bfloat16),
        compiler_params=pltpu.CompilerParams(vmem_limit_bytes=8 * MIB),
        name="pattern",
    )(place.reshape(1), disaggregation)
    base = lax.axis_index("slab") * sub + lax.axis_index("sub")
    batch = 4

    def expand(k2):
        per_part = half // batch
        return pl.pallas_call(
            functools.partial(expand_kernel, middle),
            grid_spec=pltpu.PrefetchScalarGridSpec(
                num_scalar_prefetch=1,
                grid=(per_part,),
                in_specs=[
                    pl.BlockSpec((x_half, 2 * side), lambda k, base: (0, 0)),
                    pl.BlockSpec(
                        (2, batch, count, offsets),
                        lambda k, base: (0, (2 * base[0] + k2) * per_part + k, 0, 0),
                    ),
                ],
                out_specs=pl.BlockSpec(
                    (2, batch, count, columns, 2 * LANES), lambda k, base: (0, k, 0, 0, 0)
                ),
                scratch_shapes=[
                    pltpu.VMEM((2 * LANES, x_half * LANES), jnp.bfloat16),
                    pltpu.VMEM((2 * batch * x_half, 2 * LANES), jnp.bfloat16),
                    pltpu.VMEM((2 * batch * x_half * PITCH, LANES), jnp.float32),
                ],
            ),
            out_shape=jax.ShapeDtypeStruct((2, half, count, columns, 2 * LANES), jnp.bfloat16),
            compiler_params=pltpu.CompilerParams(vmem_limit_bytes=56 * MIB),
            name="expand",
        )(base.reshape(1), index, translators)

    first = expand(0)
    across_source, first, pattern = lax.optimization_barrier((across_source, first, pattern))
    received = own, exchange(outgoing(across_source))
    expanded = first, expand(1)
    pairs = jnp.where(far_mask == 1, tile_map, middle).reshape(-1)
    steps = 4

    def translate(v):
        return pl.pallas_call(
            functools.partial(translate_kernel, wide, slab, sub, rows, columns),
            grid_spec=pltpu.PrefetchScalarGridSpec(
                num_scalar_prefetch=1,
                grid=(half // steps,),
                in_specs=[
                    pl.BlockSpec(block, lambda k, pairs: (0, 0, 0, 0, 0)),
                    pl.BlockSpec(block, lambda k, pairs: (0, 0, 0, 0, 0)),
                    pl.BlockSpec(
                        (1, steps, count, columns, 2 * LANES), lambda k, pairs: (v, k, 0, 0, 0)
                    ),
                    pl.BlockSpec(
                        (1, steps, count, columns, 2 * LANES), lambda k, pairs: (v, k, 0, 0, 0)
                    ),
                ],
                out_specs=pl.BlockSpec(block, lambda k, pairs: (0, 0, 0, 0, 0)),
            ),
            out_shape=jax.ShapeDtypeStruct(block, jnp.bfloat16),
            compiler_params=pltpu.CompilerParams(vmem_limit_bytes=50 * MIB),
            name="translate",
        )(pairs, *received, *expanded)

    def field(values, kind):
        return pl.pallas_call(
            functools.partial(field_kernel, boxes, illum),
            out_shape=jax.ShapeDtypeStruct(shape, kind),
            scratch_shapes=[
                pltpu.VMEM((near * half * PITCH, LANES), jnp.float32),
                pltpu.VMEM((boxes * PITCH, unknowns), jnp.float32),
            ],
            compiler_params=pltpu.CompilerParams(vmem_limit_bytes=12 * MIB),
            name="field",
        )(values.reshape(lines, LANES), pattern)

    far_half = exchange(translate(0))
    near_half = exchange(translate(1))
    across = cross(field(far_half, jnp.bfloat16))
    total = field(near_half, jnp.float32) + across.astype(jnp.float32)
    return total.astype(jnp.bfloat16).reshape(source.shape)


def aggregate(values, pattern_real, pattern_imag):

    def product(left_side, right_side):
        return jnp.einsum(
            "axrp,kp->krax", left_side, right_side, preferred_element_type=jnp.float32
        )

    values_real = values[:, :, 0]
    values_imag = values[:, :, 1]
    out_real = product(values_real, pattern_real) - product(values_imag, pattern_imag)
    out_imag = product(values_real, pattern_imag) + product(values_imag, pattern_real)
    return jnp.stack([out_real, out_imag], axis=1).astype(jnp.bfloat16)


def general_local(source, aggregation, translators, tile_map, far_mask, box_offsets, disaggregation):
    own_rows = source.shape[0]
    tile_count = translators.shape[2]
    offset_count = translators.shape[3]
    box_count = box_offsets.shape[0]
    target_block = 2
    block_count = own_rows // target_block
    outgoing = lax.all_to_all(
        aggregate(source, aggregation[0], aggregation[1]),
        "wide",
        split_axis=0,
        concat_axis=4,
        tiled=True,
    )
    directions_here = outgoing.shape[0]
    illum_here = outgoing.shape[2]
    row_table = jnp.concatenate(
        [translators, jnp.zeros((2, directions_here, 1, offset_count), jnp.bfloat16)], axis=2
    )
    offset_ids = lax.broadcasted_iota(jnp.int32, (offset_count, box_count, box_count), 0)
    selector = (offset_ids == box_offsets[None, :, :]).astype(jnp.bfloat16)
    selector = selector.reshape(offset_count, box_count * box_count)

    def translate(target_first, source_first, source_block):
        source_count = source_block.shape[3]
        pair_map = lax.dynamic_slice(
            tile_map, (target_first, source_first), (target_block, source_count)
        )
        pair_far = lax.dynamic_slice(
            far_mask, (target_first, source_first), (target_block, source_count)
        )
        pair_index = jnp.where(pair_far == 1, pair_map, tile_count)
        pair_rows = jnp.take(row_table, pair_index.reshape(-1), axis=2)
        expanded = jnp.dot(
            pair_rows.reshape(-1, offset_count), selector, preferred_element_type=jnp.float32
        )
        coupling = expanded.astype(jnp.bfloat16).reshape(
            2, directions_here, target_block, source_count, box_count, box_count
        )
        values = source_block.reshape(directions_here, 2 * illum_here, source_count, box_count)
        combos = jnp.einsum(
            "klcy,qkacxy->klqax", values, coupling, preferred_element_type=jnp.float32
        )
        combos = combos.reshape(directions_here, 2, illum_here, 2, target_block * box_count)
        incoming_real = combos[:, 0, :, 0] - combos[:, 1, :, 1]
        incoming_imag = combos[:, 1, :, 0] + combos[:, 0, :, 1]
        return jnp.stack([incoming_real, incoming_imag], axis=1)

    slab_first = lax.axis_index("slab") * own_rows

    def block_rows(block_index):
        return translate(block_index * target_block, slab_first, outgoing)

    summed = lax.psum_scatter(
        lax.map(block_rows, jnp.arange(block_count * lax.axis_size("slab"), dtype=jnp.int32)),
        "slab",
        scatter_dimension=0,
        tiled=True,
    )
    incoming = summed.astype(jnp.bfloat16)
    incoming = incoming.reshape(incoming.shape[:4] + (target_block, box_count))
    item_rows = lax.all_to_all(incoming, "wide", split_axis=5, concat_axis=1, tiled=True)

    def product(left_side, right_side):
        return jnp.einsum(
            "bkrax,pk->baxrp", left_side, right_side, preferred_element_type=jnp.float32
        )

    items_real = item_rows[:, :, 0]
    items_imag = item_rows[:, :, 1]
    field_real = product(items_real, disaggregation[0]) - product(items_imag, disaggregation[1])
    field_imag = product(items_real, disaggregation[1]) + product(items_imag, disaggregation[0])
    stacked = jnp.stack([field_real, field_imag], axis=3).astype(jnp.bfloat16)
    return stacked.reshape((stacked.shape[0] * stacked.shape[1],) + stacked.shape[2:])


def local(wide, slab, sub, *args):
    source, aggregation, translators, _, _, box_offsets, _ = args
    rows, columns, _, illum, unknowns = source.shape
    share = aggregation.shape[1] // (wide * slab * sub)
    tiles = (
        2 * rows * columns == LANES
        and 2 * box_offsets.shape[0] == LANES
        and columns * wide == box_offsets.shape[0]
        and slab == 2
        and wide == 4
        and columns == 16
        and illum == 16
        and share % 32 == 0
        and unknowns == LANES
        and LANES < translators.shape[3] <= 2 * LANES
        and translators.shape[2] <= 32
    )
    if tiles:
        return tiled_local(wide, slab, sub, *args)
    return general_local(*args)


def solution(mesh):
    placed = (
        P(("groups", "slab"), "wide", None, "sub", None),
        P(None, "groups", None),
        P(None, ("groups", "wide"), None, None),
        P(),
        P(),
        P(),
        P(None, None, "groups"),
    )
    return jax.shard_map(
        functools.partial(local, mesh.shape["wide"], mesh.shape["slab"], mesh.shape["sub"]),
        mesh=mesh,
        in_specs=placed,
        out_specs=P(("groups", "slab"), "wide", None, "sub", None),
        check_vma=False,
    )
```

```python
import functools

import jax
import jax.numpy as jnp
from jax import lax
from jax.experimental import pallas as pl
from jax.experimental.pallas import tpu as pltpu
from jax.sharding import PartitionSpec as P

OWNERS = ("wide", "slab", "sub")
LANES = 128
MIB = 1024 * 1024
PITCH = 36
NT = (((1,), (1,)), ((), ()))
TN = (((0,), (0,)), ((), ()))


def outgoing_kernel(boxes, illum, devices, half, place_ref, src_ref, agg_ref, out_ref, wide_src, wide_out):
    unknowns = src_ref.shape[1]
    wide_src[...] = src_ref[...].astype(jnp.float32)
    real = agg_ref[0].astype(jnp.float32)
    imag = agg_ref[1].astype(jnp.float32)

    def pick(array, part):
        return jnp.concatenate(
            [array[(2 * d + part) * half:(2 * d + part + 1) * half] for d in range(devices)], axis=0
        )

    real_low, real_high = pick(real, 0), pick(real, 1)
    imag_low, imag_high = pick(imag, 0), pick(imag, 1)
    to_real = jnp.concatenate([real_low, -imag_low, real_high, -imag_high], axis=1).astype(jnp.bfloat16)
    to_imag = jnp.concatenate([imag_low, real_low, imag_high, real_high], axis=1).astype(jnp.bfloat16)
    zeros = jnp.zeros((boxes, 2 * unknowns), jnp.bfloat16)
    rows = devices * half
    for r in range(illum):
        both = jnp.concatenate(
            [wide_src[pl.ds(q * illum + r, boxes, stride=2 * illum), :] for q in range(2)], axis=1
        ).astype(jnp.bfloat16)
        right = jnp.concatenate(
            [jnp.concatenate([both, zeros], axis=1), jnp.concatenate([zeros, both], axis=1)], axis=0
        )
        for q, left in ((0, to_real), (1, to_imag)):
            wide_out[pl.ds(q * illum + r, rows, stride=PITCH), :] = lax.dot_general(
                left, right, NT, preferred_element_type=jnp.float32
            )
    tall = 2 * illum
    for g in range(rows):
        out_ref[g * tall:(g + 1) * tall] = wide_out[g * PITCH:g * PITCH + tall].astype(jnp.bfloat16)


def expand_kernel(middle, base_ref, index_ref, table_ref, out_ref, choice, left, wide):
    batch, translators, offsets = table_ref.shape[1:]
    depth = out_ref.shape[3]
    tall = 2 * depth
    rows = 2 * batch * tall

    @pl.when(pl.program_id(0) == 0)
    def _():
        offset = lax.broadcasted_iota(jnp.int32, (2 * LANES, LANES), 0)
        for x in range(tall):
            choice[:, x * LANES:(x + 1) * LANES] = jnp.where(
                offset == index_ref[x:x + 1, :], 1.0, 0.0
            ).astype(jnp.bfloat16)
        left[...] = jnp.zeros_like(left)

    for q in range(2):
        for k in range(batch):
            row = (q * batch + k) * tall
            left[row:row + translators, 0:offsets] = table_ref[q, k]
    table = left[...]
    for x in range(0, tall, 2):
        picked = jnp.dot(
            table, choice[:, x * LANES:(x + 2) * LANES], preferred_element_type=jnp.float32
        )
        wide[pl.ds(x, rows, stride=PITCH), :] = picked[:, :LANES]
        wide[pl.ds(x + 1, rows, stride=PITCH), :] = picked[:, LANES:]
    for k in range(batch):
        for v in range(2):
            out_ref[v, k, middle] = jnp.zeros(out_ref.shape[3:], jnp.bfloat16)
        for t in range(translators):
            if abs(t - middle) < 2:
                continue
            for q in range(2):
                row = ((q * batch + k) * tall + t) * PITCH
                for v in range(2):
                    out_ref[v, k, t, :, q * LANES:(q + 1) * LANES] = wide[
                        row + v * depth:row + (v + 1) * depth
                    ].astype(jnp.bfloat16)


def translate_kernel(wide, slab, sub, rows, columns, pair_ref, own_ref, far_ref, low_ref, high_ref, out_ref):
    illum = own_ref.shape[3]
    steps = low_ref.shape[1]
    all_rows = slab * rows
    lane = lax.broadcasted_iota(jnp.int32, (illum, LANES), 1)
    group = lane // columns
    groups = LANES // columns
    lower = lane < LANES // 2
    zero = jnp.zeros((illum, LANES), jnp.bfloat16)
    for step in range(steps):
        here = pl.program_id(0) * steps + step
        sums = [None, None]
        turned = {}

        def turn(s, u, q, w, amount):
            key = (s, u, q, w, amount)
            if key not in turned:
                tile = (own_ref, far_ref)[w // 2][(w % 2 * slab + s) * sub + u, here, q]
                turned[key] = pltpu.roll(tile, amount * columns, 1) if amount else tile
            return turned[key]

        for c in range(all_rows):
            s, own = c // rows, c % rows
            for k2 in range(2):
                position = k2 * rows + own
                parts = {}
                for u in range(sub):
                    for q in range(2):
                        for h in range(2):
                            tile = zero
                            for w in range(wide):
                                place = h * wide + w
                                tile = jnp.where(
                                    group == place,
                                    turn(s, u, q, w, (place - position) % groups),
                                    tile,
                                )
                            parts[u, q, h] = tile
                left = []
                for h in range(2):
                    for u in range(sub):
                        left.append(jnp.concatenate([parts[u, 0, h], -parts[u, 1, h]], axis=1))
                        left.append(jnp.concatenate([parts[u, 1, h], parts[u, 0, h]], axis=1))
                left = jnp.concatenate(left, axis=0)
                right = jnp.concatenate(
                    [
                        (low_ref, high_ref)[k2][0, step, pair_ref[a * all_rows + c]]
                        for a in range(all_rows)
                    ],
                    axis=0,
                )
                product = lax.dot_general(left, right, NT, preferred_element_type=jnp.float32)
                sums[k2] = product if sums[k2] is None else sums[k2] + product
        for h in range(2):
            for u in range(sub):
                for q in range(2):
                    row = ((h * sub + u) * 2 + q) * illum
                    first = sums[0][row:row + illum]
                    second = sums[1][row:row + illum]
                    for s in range(slab):
                        if s == 0:
                            tile = jnp.where(lower, first, pltpu.roll(second, LANES // 2, 1))
                        else:
                            tile = jnp.where(lower, pltpu.roll(first, LANES // 2, 1), second)
                        out_ref[(h * slab + s) * sub + u, here, q] = tile.astype(jnp.bfloat16)


def pattern_kernel(devices, half, place_ref, dis_ref, out_ref):
    real = dis_ref[0].astype(jnp.float32).T
    imag = dis_ref[1].astype(jnp.float32).T

    def pick(array, part):
        return jnp.concatenate(
            [array[(2 * d + part) * half:(2 * d + part + 1) * half] for d in range(devices)], axis=0
        )

    sides = []
    for part in range(2):
        real_part, imag_part = pick(real, part), pick(imag, part)
        sides.append(
            jnp.concatenate(
                [
                    jnp.concatenate([real_part, imag_part], axis=1),
                    jnp.concatenate([-imag_part, real_part], axis=1),
                ],
                axis=0,
            )
        )
    out_ref[...] = jnp.concatenate(sides, axis=1).astype(jnp.bfloat16)


def field_kernel(boxes, illum, inc_ref, pattern_ref, out_ref, wide_inc, wide_out):
    unknowns = out_ref.shape[1]
    tall = 2 * illum
    rows = inc_ref.shape[0] // tall
    for g in range(rows):
        wide_inc[g * PITCH:g * PITCH + tall] = inc_ref[g * tall:(g + 1) * tall].astype(jnp.float32)
    right = pattern_ref[...]
    for r in range(illum):
        left = jnp.concatenate(
            [wide_inc[pl.ds(q * illum + r, rows, stride=PITCH), :] for q in range(2)], axis=0
        ).astype(jnp.bfloat16)
        product = lax.dot_general(left, right, TN, preferred_element_type=jnp.float32)
        total = product[:boxes, :2 * unknowns] + product[boxes:, 2 * unknowns:]
        for q in range(2):
            wide_out[pl.ds(q * illum + r, boxes, stride=PITCH), :] = total[
                :, q * unknowns:(q + 1) * unknowns
            ]
    for g in range(boxes):
        out_ref[g * tall:(g + 1) * tall] = wide_out[g * PITCH:g * PITCH + tall].astype(out_ref.dtype)


def tiled_local(wide, slab, sub, source, aggregation, translators, tile_map, far_mask, box_offsets, disaggregation):
    rows, columns, _, illum, unknowns = source.shape
    devices = wide * slab * sub
    directions = aggregation.shape[1]
    half = directions // devices // 2
    boxes = rows * columns
    all_rows = slab * rows
    count = translators.shape[2]
    offsets = translators.shape[3]
    middle = count // 2

    near = devices // 2
    lines = near * half * 2 * illum
    block = (near, half, 2, illum, LANES)
    shape = (boxes * 2 * illum, unknowns)
    place = lax.axis_index("wide") // 2
    neighbours = [[first * near + d for d in range(near)] for first in range(2)]

    def exchange(values):
        return lax.all_to_all(
            values, OWNERS, split_axis=0, concat_axis=0, tiled=True, axis_index_groups=neighbours
        )

    def cross(values):
        return lax.ppermute(values, "wide", [(w, (w + wide // 2) % wide) for w in range(wide)])

    def outgoing(values, limit):
        return pl.pallas_call(
            functools.partial(outgoing_kernel, boxes, illum, near, half),
            grid_spec=pltpu.PrefetchScalarGridSpec(
                num_scalar_prefetch=1,
                grid=(1,),
                in_specs=[
                    pl.BlockSpec(shape, lambda i, place: (0, 0)),
                    pl.BlockSpec((2, directions // 2, unknowns), lambda i, place: (0, place[0], 0)),
                ],
                out_specs=pl.BlockSpec((lines, LANES), lambda i, place: (0, 0)),
                scratch_shapes=[
                    pltpu.VMEM(shape, jnp.float32),
                    pltpu.VMEM((near * half * PITCH, LANES), jnp.float32),
                ],
            ),
            out_shape=jax.ShapeDtypeStruct((lines, LANES), jnp.bfloat16),
            compiler_params=pltpu.CompilerParams(vmem_limit_bytes=limit * MIB),
            name="outgoing",
        )(place.reshape(1), values, aggregation).reshape(block)

    flat = source.reshape(shape)
    across_source = cross(flat)
    own = exchange(outgoing(flat, 56))

    side = box_offsets.shape[0]
    x_half = side // 2
    by_side = jnp.roll(box_offsets, x_half, axis=0)
    by_side = jnp.where(place == 0, by_side, jnp.roll(box_offsets, x_half, axis=1))
    by_side = by_side.reshape(2, 2, columns, side)
    index = jnp.concatenate([by_side[:, 0], by_side[:, 1]], axis=-1).reshape(x_half, 2 * side)
    base = lax.axis_index("slab") * sub + lax.axis_index("sub")
    pattern = pl.pallas_call(
        functools.partial(pattern_kernel, near, half),
        grid_spec=pltpu.PrefetchScalarGridSpec(
            num_scalar_prefetch=1,
            grid=(1,),
            in_specs=[pl.BlockSpec((2, unknowns, directions // 2), lambda i, place: (0, 0, place[0]))],
            out_specs=pl.BlockSpec((2 * near * half, 4 * unknowns), lambda i, place: (0, 0)),
        ),
        out_shape=jax.ShapeDtypeStruct((2 * near * half, 4 * unknowns), jnp.bfloat16),
        compiler_params=pltpu.CompilerParams(vmem_limit_bytes=8 * MIB),
        name="pattern",
    )(place.reshape(1), disaggregation)
    base = lax.axis_index("slab") * sub + lax.axis_index("sub")
    batch = 4

    def expand(k2):
        per_part = half // batch
        return pl.pallas_call(
            functools.partial(expand_kernel, middle),
            grid_spec=pltpu.PrefetchScalarGridSpec(
                num_scalar_prefetch=1,
                grid=(per_part,),
                in_specs=[
                    pl.BlockSpec((x_half, 2 * side), lambda k, base: (0, 0)),
                    pl.BlockSpec(
                        (2, batch, count, offsets),
                        lambda k, base: (0, (2 * base[0] + k2) * per_part + k, 0, 0),
                    ),
                ],
                out_specs=pl.BlockSpec(
                    (2, batch, count, columns, 2 * LANES), lambda k, base: (0, k, 0, 0, 0)
                ),
                scratch_shapes=[
                    pltpu.VMEM((2 * LANES, x_half * LANES), jnp.bfloat16),
                    pltpu.VMEM((2 * batch * x_half, 2 * LANES), jnp.bfloat16),
                    pltpu.VMEM((2 * batch * x_half * PITCH, LANES), jnp.float32),
                ],
            ),
            out_shape=jax.ShapeDtypeStruct((2, half, count, columns, 2 * LANES), jnp.bfloat16),
            compiler_params=pltpu.CompilerParams(vmem_limit_bytes=56 * MIB),
            cost_estimate=pl.CostEstimate(
                flops=8 * 2 * 2 * half * x_half * 2 * LANES * x_half * LANES,
                bytes_accessed=8 * 2 * half * count * columns * 2 * LANES * 2,
                transcendentals=0,
            ),
            name="expand",
        )(base.reshape(1), index, translators)

    first = expand(0)
    across_source, first, pattern = lax.optimization_barrier((across_source, first, pattern))
    received = own, exchange(outgoing(across_source, 16))
    expanded = first, expand(1)
    pairs = jnp.where(far_mask == 1, tile_map, middle).reshape(-1)
    steps = 4

    def translate(v):
        return pl.pallas_call(
            functools.partial(translate_kernel, wide, slab, sub, rows, columns),
            grid_spec=pltpu.PrefetchScalarGridSpec(
                num_scalar_prefetch=1,
                grid=(half // steps,),
                in_specs=[
                    pl.BlockSpec(block, lambda k, pairs: (0, 0, 0, 0, 0)),
                    pl.BlockSpec(block, lambda k, pairs: (0, 0, 0, 0, 0)),
                    pl.BlockSpec(
                        (1, steps, count, columns, 2 * LANES), lambda k, pairs: (v, k, 0, 0, 0)
                    ),
                    pl.BlockSpec(
                        (1, steps, count, columns, 2 * LANES), lambda k, pairs: (v, k, 0, 0, 0)
                    ),
                ],
                out_specs=pl.BlockSpec(block, lambda k, pairs: (0, 0, 0, 0, 0)),
            ),
            out_shape=jax.ShapeDtypeStruct(block, jnp.bfloat16),
            compiler_params=pltpu.CompilerParams(vmem_limit_bytes=50 * MIB),
            name="translate",
        )(pairs, *received, *expanded)

    def field(values, kind):
        return pl.pallas_call(
            functools.partial(field_kernel, boxes, illum),
            out_shape=jax.ShapeDtypeStruct(shape, kind),
            scratch_shapes=[
                pltpu.VMEM((near * half * PITCH, LANES), jnp.float32),
                pltpu.VMEM((boxes * PITCH, unknowns), jnp.float32),
            ],
            compiler_params=pltpu.CompilerParams(vmem_limit_bytes=12 * MIB),
            name="field",
        )(values.reshape(lines, LANES), pattern)

    far_half = exchange(translate(0))
    near_half = exchange(translate(1))
    across = cross(field(far_half, jnp.bfloat16))
    total = field(near_half, jnp.float32) + across.astype(jnp.float32)
    return total.astype(jnp.bfloat16).reshape(source.shape)


def aggregate(values, pattern_real, pattern_imag):

    def product(left_side, right_side):
        return jnp.einsum(
            "axrp,kp->krax", left_side, right_side, preferred_element_type=jnp.float32
        )

    values_real = values[:, :, 0]
    values_imag = values[:, :, 1]
    out_real = product(values_real, pattern_real) - product(values_imag, pattern_imag)
    out_imag = product(values_real, pattern_imag) + product(values_imag, pattern_real)
    return jnp.stack([out_real, out_imag], axis=1).astype(jnp.bfloat16)


def general_local(source, aggregation, translators, tile_map, far_mask, box_offsets, disaggregation):
    own_rows = source.shape[0]
    tile_count = translators.shape[2]
    offset_count = translators.shape[3]
    box_count = box_offsets.shape[0]
    target_block = 2
    block_count = own_rows // target_block
    outgoing = lax.all_to_all(
        aggregate(source, aggregation[0], aggregation[1]),
        "wide",
        split_axis=0,
        concat_axis=4,
        tiled=True,
    )
    directions_here = outgoing.shape[0]
    illum_here = outgoing.shape[2]
    row_table = jnp.concatenate(
        [translators, jnp.zeros((2, directions_here, 1, offset_count), jnp.bfloat16)], axis=2
    )
    offset_ids = lax.broadcasted_iota(jnp.int32, (offset_count, box_count, box_count), 0)
    selector = (offset_ids == box_offsets[None, :, :]).astype(jnp.bfloat16)
    selector = selector.reshape(offset_count, box_count * box_count)

    def translate(target_first, source_first, source_block):
        source_count = source_block.shape[3]
        pair_map = lax.dynamic_slice(
            tile_map, (target_first, source_first), (target_block, source_count)
        )
        pair_far = lax.dynamic_slice(
            far_mask, (target_first, source_first), (target_block, source_count)
        )
        pair_index = jnp.where(pair_far == 1, pair_map, tile_count)
        pair_rows = jnp.take(row_table, pair_index.reshape(-1), axis=2)
        expanded = jnp.dot(
            pair_rows.reshape(-1, offset_count), selector, preferred_element_type=jnp.float32
        )
        coupling = expanded.astype(jnp.bfloat16).reshape(
            2, directions_here, target_block, source_count, box_count, box_count
        )
        values = source_block.reshape(directions_here, 2 * illum_here, source_count, box_count)
        combos = jnp.einsum(
            "klcy,qkacxy->klqax", values, coupling, preferred_element_type=jnp.float32
        )
        combos = combos.reshape(directions_here, 2, illum_here, 2, target_block * box_count)
        incoming_real = combos[:, 0, :, 0] - combos[:, 1, :, 1]
        incoming_imag = combos[:, 1, :, 0] + combos[:, 0, :, 1]
        return jnp.stack([incoming_real, incoming_imag], axis=1)

    slab_first = lax.axis_index("slab") * own_rows

    def block_rows(block_index):
        return translate(block_index * target_block, slab_first, outgoing)

    summed = lax.psum_scatter(
        lax.map(block_rows, jnp.arange(block_count * lax.axis_size("slab"), dtype=jnp.int32)),
        "slab",
        scatter_dimension=0,
        tiled=True,
    )
    incoming = summed.astype(jnp.bfloat16)
    incoming = incoming.reshape(incoming.shape[:4] + (target_block, box_count))
    item_rows = lax.all_to_all(incoming, "wide", split_axis=5, concat_axis=1, tiled=True)

    def product(left_side, right_side):
        return jnp.einsum(
            "bkrax,pk->baxrp", left_side, right_side, preferred_element_type=jnp.float32
        )

    items_real = item_rows[:, :, 0]
    items_imag = item_rows[:, :, 1]
    field_real = product(items_real, disaggregation[0]) - product(items_imag, disaggregation[1])
    field_imag = product(items_real, disaggregation[1]) + product(items_imag, disaggregation[0])
    stacked = jnp.stack([field_real, field_imag], axis=3).astype(jnp.bfloat16)
    return stacked.reshape((stacked.shape[0] * stacked.shape[1],) + stacked.shape[2:])


def local(wide, slab, sub, *args):
    source, aggregation, translators, _, _, box_offsets, _ = args
    rows, columns, _, illum, unknowns = source.shape
    share = aggregation.shape[1] // (wide * slab * sub)
    tiles = (
        2 * rows * columns == LANES
        and 2 * box_offsets.shape[0] == LANES
        and columns * wide == box_offsets.shape[0]
        and slab == 2
        and wide == 4
        and columns == 16
        and illum == 16
        and share % 32 == 0
        and unknowns == LANES
        and LANES < translators.shape[3] <= 2 * LANES
        and translators.shape[2] <= 32
    )
    if tiles:
        return tiled_local(wide, slab, sub, *args)
    return general_local(*args)


def solution(mesh):
    placed = (
        P(("groups", "slab"), "wide", None, "sub", None),
        P(None, "groups", None),
        P(None, ("groups", "wide"), None, None),
        P(),
        P(),
        P(),
        P(None, None, "groups"),
    )
    return jax.shard_map(
        functools.partial(local, mesh.shape["wide"], mesh.shape["slab"], mesh.shape["sub"]),
        mesh=mesh,
        in_specs=placed,
        out_specs=P(("groups", "slab"), "wide", None, "sub", None),
        check_vma=False,
    )
```

```python
import functools

import jax
import jax.numpy as jnp
from jax import lax
from jax.experimental import pallas as pl
from jax.experimental.pallas import tpu as pltpu
from jax.sharding import PartitionSpec as P

OWNERS = ("wide", "slab", "sub")
LANES = 128
MIB = 1024 * 1024
PITCH = 36
SPARE = 40
NT = (((1,), (1,)), ((), ()))
TN = (((0,), (0,)), ((), ()))


def outgoing_kernel(boxes, illum, devices, half, place_ref, src_ref, agg_ref, out_ref, wide_src, wide_out):
    unknowns = src_ref.shape[1]
    wide_src[0:src_ref.shape[0]] = src_ref[...].astype(jnp.float32)
    real = agg_ref[0].astype(jnp.float32)
    imag = agg_ref[1].astype(jnp.float32)

    def pick(array, part):
        return jnp.concatenate(
            [array[(2 * d + part) * half:(2 * d + part + 1) * half] for d in range(devices)], axis=0
        )

    real_low, real_high = pick(real, 0), pick(real, 1)
    imag_low, imag_high = pick(imag, 0), pick(imag, 1)
    to_real = jnp.concatenate([real_low, -imag_low, real_high, -imag_high], axis=1).astype(jnp.bfloat16)
    to_imag = jnp.concatenate([imag_low, real_low, imag_high, real_high], axis=1).astype(jnp.bfloat16)
    zeros = jnp.zeros((boxes, 2 * unknowns), jnp.bfloat16)
    rows = devices * half
    for r in range(illum):
        both = jnp.concatenate(
            [wide_src[pl.ds(q * illum + r, boxes, stride=2 * illum), :] for q in range(2)], axis=1
        ).astype(jnp.bfloat16)
        right = jnp.concatenate(
            [jnp.concatenate([both, zeros], axis=1), jnp.concatenate([zeros, both], axis=1)], axis=0
        )
        for q, left in ((0, to_real), (1, to_imag)):
            wide_out[pl.ds(q * illum + r, rows, stride=PITCH), :] = lax.dot_general(
                left, right, NT, preferred_element_type=jnp.float32
            )
    tall = 2 * illum
    for g in range(rows):
        out_ref[g * tall:(g + 1) * tall] = wide_out[g * PITCH:g * PITCH + tall].astype(jnp.bfloat16)


def expand_kernel(middle, base_ref, index_ref, table_ref, out_ref, choice, left, wide):
    batch, translators, offsets = table_ref.shape[1:]
    depth = out_ref.shape[3]
    tall = 2 * depth
    rows = 2 * batch * tall

    @pl.when(pl.program_id(0) == 0)
    def _():
        offset = lax.broadcasted_iota(jnp.int32, (2 * LANES, LANES), 0)
        for x in range(tall):
            choice[:, x * LANES:(x + 1) * LANES] = jnp.where(
                offset == index_ref[x:x + 1, :], 1.0, 0.0
            ).astype(jnp.bfloat16)
        left[...] = jnp.zeros_like(left)

    for q in range(2):
        for k in range(batch):
            row = (q * batch + k) * tall
            left[row:row + translators, 0:offsets] = table_ref[q, k]
    table = left[...]
    for x in range(0, tall, 2):
        picked = jnp.dot(
            table, choice[:, x * LANES:(x + 2) * LANES], preferred_element_type=jnp.float32
        )
        wide[pl.ds(x, rows, stride=PITCH), :] = picked[:, :LANES]
        wide[pl.ds(x + 1, rows, stride=PITCH), :] = picked[:, LANES:]
    for k in range(batch):
        for v in range(2):
            out_ref[v, k, middle] = jnp.zeros(out_ref.shape[3:], jnp.bfloat16)
        for t in range(translators):
            if abs(t - middle) < 2:
                continue
            for q in range(2):
                row = ((q * batch + k) * tall + t) * PITCH
                for v in range(2):
                    out_ref[v, k, t, :, q * LANES:(q + 1) * LANES] = wide[
                        row + v * depth:row + (v + 1) * depth
                    ].astype(jnp.bfloat16)


def translate_kernel(wide, slab, sub, rows, columns, pair_ref, own_ref, far_ref, low_ref, high_ref, out_ref):
    illum = own_ref.shape[3]
    steps = low_ref.shape[1]
    all_rows = slab * rows
    lane = lax.broadcasted_iota(jnp.int32, (illum, LANES), 1)
    group = lane // columns
    groups = LANES // columns
    lower = lane < LANES // 2
    zero = jnp.zeros((illum, LANES), jnp.bfloat16)
    for step in range(steps):
        here = pl.program_id(0) * steps + step
        sums = [None, None]
        turned = {}

        def turn(s, u, q, w, amount):
            key = (s, u, q, w, amount)
            if key not in turned:
                tile = (own_ref, far_ref)[w // 2][(w % 2 * slab + s) * sub + u, here, q]
                turned[key] = pltpu.roll(tile, amount * columns, 1) if amount else tile
            return turned[key]

        for c in range(all_rows):
            s, own = c // rows, c % rows
            for k2 in range(2):
                position = k2 * rows + own
                parts = {}
                for u in range(sub):
                    for q in range(2):
                        for h in range(2):
                            tile = zero
                            for w in range(wide):
                                place = h * wide + w
                                tile = jnp.where(
                                    group == place,
                                    turn(s, u, q, w, (place - position) % groups),
                                    tile,
                                )
                            parts[u, q, h] = tile
                left = []
                for h in range(2):
                    for u in range(sub):
                        left.append(jnp.concatenate([parts[u, 0, h], -parts[u, 1, h]], axis=1))
                        left.append(jnp.concatenate([parts[u, 1, h], parts[u, 0, h]], axis=1))
                left = jnp.concatenate(left, axis=0)
                right = jnp.concatenate(
                    [
                        (low_ref, high_ref)[k2][0, step, pair_ref[a * all_rows + c]]
                        for a in range(all_rows)
                    ],
                    axis=0,
                )
                product = lax.dot_general(left, right, NT, preferred_element_type=jnp.float32)
                sums[k2] = product if sums[k2] is None else sums[k2] + product
        for h in range(2):
            for u in range(sub):
                for q in range(2):
                    row = ((h * sub + u) * 2 + q) * illum
                    first = sums[0][row:row + illum]
                    second = sums[1][row:row + illum]
                    for s in range(slab):
                        if s == 0:
                            tile = jnp.where(lower, first, pltpu.roll(second, LANES // 2, 1))
                        else:
                            tile = jnp.where(lower, pltpu.roll(first, LANES // 2, 1), second)
                        out_ref[(h * slab + s) * sub + u, here, q] = tile.astype(jnp.bfloat16)


def pattern_kernel(devices, half, place_ref, dis_ref, out_ref):
    real = dis_ref[0].astype(jnp.float32).T
    imag = dis_ref[1].astype(jnp.float32).T

    def pick(array, part):
        return jnp.concatenate(
            [array[(2 * d + part) * half:(2 * d + part + 1) * half] for d in range(devices)], axis=0
        )

    sides = []
    for part in range(2):
        real_part, imag_part = pick(real, part), pick(imag, part)
        sides.append(
            jnp.concatenate(
                [
                    jnp.concatenate([real_part, imag_part], axis=1),
                    jnp.concatenate([-imag_part, real_part], axis=1),
                ],
                axis=0,
            )
        )
    out_ref[...] = jnp.concatenate(sides, axis=1).astype(jnp.bfloat16)


def field_kernel(boxes, illum, inc_ref, pattern_ref, out_ref, wide_inc, wide_out):
    unknowns = out_ref.shape[1]
    tall = 2 * illum
    rows = inc_ref.shape[0] // tall
    for g in range(rows):
        wide_inc[g * PITCH:g * PITCH + tall] = inc_ref[g * tall:(g + 1) * tall].astype(jnp.float32)
    right = pattern_ref[...]
    for r in range(illum):
        left = jnp.concatenate(
            [wide_inc[pl.ds(q * illum + r, rows, stride=PITCH), :] for q in range(2)], axis=0
        ).astype(jnp.bfloat16)
        product = lax.dot_general(left, right, TN, preferred_element_type=jnp.float32)
        total = product[:boxes, :2 * unknowns] + product[boxes:, 2 * unknowns:]
        for q in range(2):
            wide_out[pl.ds(q * illum + r, boxes, stride=PITCH), :] = total[
                :, q * unknowns:(q + 1) * unknowns
            ]
    for g in range(boxes):
        out_ref[g * tall:(g + 1) * tall] = wide_out[g * PITCH:g * PITCH + tall].astype(out_ref.dtype)


def tiled_local(wide, slab, sub, source, aggregation, translators, tile_map, far_mask, box_offsets, disaggregation):
    rows, columns, _, illum, unknowns = source.shape
    devices = wide * slab * sub
    directions = aggregation.shape[1]
    half = directions // devices // 2
    boxes = rows * columns
    all_rows = slab * rows
    count = translators.shape[2]
    offsets = translators.shape[3]
    middle = count // 2

    near = devices // 2
    lines = near * half * 2 * illum
    block = (near, half, 2, illum, LANES)
    shape = (boxes * 2 * illum, unknowns)
    place = lax.axis_index("wide") // 2
    neighbours = [[first * near + d for d in range(near)] for first in range(2)]

    def exchange(values):
        return lax.all_to_all(
            values, OWNERS, split_axis=0, concat_axis=0, tiled=True, axis_index_groups=neighbours
        )

    def cross(values):
        return lax.ppermute(values, "wide", [(w, (w + wide // 2) % wide) for w in range(wide)])

    def outgoing(values, limit):
        return pl.pallas_call(
            functools.partial(outgoing_kernel, boxes, illum, near, half),
            grid_spec=pltpu.PrefetchScalarGridSpec(
                num_scalar_prefetch=1,
                grid=(1,),
                in_specs=[
                    pl.BlockSpec(shape, lambda i, place: (0, 0)),
                    pl.BlockSpec((2, directions // 2, unknowns), lambda i, place: (0, place[0], 0)),
                ],
                out_specs=pl.BlockSpec((lines, LANES), lambda i, place: (0, 0)),
                scratch_shapes=[
                    pltpu.VMEM((shape[0] + SPARE, unknowns), jnp.float32),
                    pltpu.VMEM((near * half * PITCH + SPARE, LANES), jnp.float32),
                ],
            ),
            out_shape=jax.ShapeDtypeStruct((lines, LANES), jnp.bfloat16),
            compiler_params=pltpu.CompilerParams(vmem_limit_bytes=limit * MIB),
            name="outgoing",
        )(place.reshape(1), values, aggregation).reshape(block)

    flat = source.reshape(shape)
    across_source = cross(flat)
    own = exchange(outgoing(flat, 56))

    side = box_offsets.shape[0]
    x_half = side // 2
    by_side = jnp.roll(box_offsets, x_half, axis=0)
    by_side = jnp.where(place == 0, by_side, jnp.roll(box_offsets, x_half, axis=1))
    by_side = by_side.reshape(2, 2, columns, side)
    index = jnp.concatenate([by_side[:, 0], by_side[:, 1]], axis=-1).reshape(x_half, 2 * side)
    base = lax.axis_index("slab") * sub + lax.axis_index("sub")
    pattern = pl.pallas_call(
        functools.partial(pattern_kernel, near, half),
        grid_spec=pltpu.PrefetchScalarGridSpec(
            num_scalar_prefetch=1,
            grid=(1,),
            in_specs=[pl.BlockSpec((2, unknowns, directions // 2), lambda i, place: (0, 0, place[0]))],
            out_specs=pl.BlockSpec((2 * near * half, 4 * unknowns), lambda i, place: (0, 0)),
        ),
        out_shape=jax.ShapeDtypeStruct((2 * near * half, 4 * unknowns), jnp.bfloat16),
        compiler_params=pltpu.CompilerParams(vmem_limit_bytes=8 * MIB),
        name="pattern",
    )(place.reshape(1), disaggregation)
    base = lax.axis_index("slab") * sub + lax.axis_index("sub")
    batch = 4

    def expand(k2):
        per_part = half // batch
        return pl.pallas_call(
            functools.partial(expand_kernel, middle),
            grid_spec=pltpu.PrefetchScalarGridSpec(
                num_scalar_prefetch=1,
                grid=(per_part,),
                in_specs=[
                    pl.BlockSpec((x_half, 2 * side), lambda k, base: (0, 0)),
                    pl.BlockSpec(
                        (2, batch, count, offsets),
                        lambda k, base: (0, (2 * base[0] + k2) * per_part + k, 0, 0),
                    ),
                ],
                out_specs=pl.BlockSpec(
                    (2, batch, count, columns, 2 * LANES), lambda k, base: (0, k, 0, 0, 0)
                ),
                scratch_shapes=[
                    pltpu.VMEM((2 * LANES, x_half * LANES), jnp.bfloat16),
                    pltpu.VMEM((2 * batch * x_half, 2 * LANES), jnp.bfloat16),
                    pltpu.VMEM((2 * batch * x_half * PITCH + SPARE, LANES), jnp.float32),
                ],
            ),
            out_shape=jax.ShapeDtypeStruct((2, half, count, columns, 2 * LANES), jnp.bfloat16),
            compiler_params=pltpu.CompilerParams(vmem_limit_bytes=56 * MIB),
            cost_estimate=pl.CostEstimate(
                flops=8 * 2 * 2 * half * x_half * 2 * LANES * x_half * LANES,
                bytes_accessed=8 * 2 * half * count * columns * 2 * LANES * 2,
                transcendentals=0,
            ),
            name="expand",
        )(base.reshape(1), index, translators)

    first = expand(0)
    across_source, first, pattern = lax.optimization_barrier((across_source, first, pattern))
    received = own, exchange(outgoing(across_source, 16))
    expanded = first, expand(1)
    pairs = jnp.where(far_mask == 1, tile_map, middle).reshape(-1)
    steps = 4

    def translate(v):
        return pl.pallas_call(
            functools.partial(translate_kernel, wide, slab, sub, rows, columns),
            grid_spec=pltpu.PrefetchScalarGridSpec(
                num_scalar_prefetch=1,
                grid=(half // steps,),
                in_specs=[
                    pl.BlockSpec(block, lambda k, pairs: (0, 0, 0, 0, 0)),
                    pl.BlockSpec(block, lambda k, pairs: (0, 0, 0, 0, 0)),
                    pl.BlockSpec(
                        (1, steps, count, columns, 2 * LANES), lambda k, pairs: (v, k, 0, 0, 0)
                    ),
                    pl.BlockSpec(
                        (1, steps, count, columns, 2 * LANES), lambda k, pairs: (v, k, 0, 0, 0)
                    ),
                ],
                out_specs=pl.BlockSpec(block, lambda k, pairs: (0, 0, 0, 0, 0)),
            ),
            out_shape=jax.ShapeDtypeStruct(block, jnp.bfloat16),
            compiler_params=pltpu.CompilerParams(vmem_limit_bytes=50 * MIB),
            name="translate",
        )(pairs, *received, *expanded)

    def field(values, kind):
        return pl.pallas_call(
            functools.partial(field_kernel, boxes, illum),
            out_shape=jax.ShapeDtypeStruct(shape, kind),
            scratch_shapes=[
                pltpu.VMEM((near * half * PITCH + SPARE, LANES), jnp.float32),
                pltpu.VMEM((boxes * PITCH + SPARE, unknowns), jnp.float32),
            ],
            compiler_params=pltpu.CompilerParams(vmem_limit_bytes=12 * MIB),
            name="field",
        )(values.reshape(lines, LANES), pattern)

    far_half = exchange(translate(0))
    near_half = exchange(translate(1))
    across = cross(field(far_half, jnp.bfloat16))
    total = field(near_half, jnp.float32) + across.astype(jnp.float32)
    return total.astype(jnp.bfloat16).reshape(source.shape)


def aggregate(values, pattern_real, pattern_imag):

    def product(left_side, right_side):
        return jnp.einsum(
            "axrp,kp->krax", left_side, right_side, preferred_element_type=jnp.float32
        )

    values_real = values[:, :, 0]
    values_imag = values[:, :, 1]
    out_real = product(values_real, pattern_real) - product(values_imag, pattern_imag)
    out_imag = product(values_real, pattern_imag) + product(values_imag, pattern_real)
    return jnp.stack([out_real, out_imag], axis=1).astype(jnp.bfloat16)


def general_local(source, aggregation, translators, tile_map, far_mask, box_offsets, disaggregation):
    own_rows = source.shape[0]
    tile_count = translators.shape[2]
    offset_count = translators.shape[3]
    box_count = box_offsets.shape[0]
    target_block = 2
    block_count = own_rows // target_block
    outgoing = lax.all_to_all(
        aggregate(source, aggregation[0], aggregation[1]),
        "wide",
        split_axis=0,
        concat_axis=4,
        tiled=True,
    )
    directions_here = outgoing.shape[0]
    illum_here = outgoing.shape[2]
    row_table = jnp.concatenate(
        [translators, jnp.zeros((2, directions_here, 1, offset_count), jnp.bfloat16)], axis=2
    )
    offset_ids = lax.broadcasted_iota(jnp.int32, (offset_count, box_count, box_count), 0)
    selector = (offset_ids == box_offsets[None, :, :]).astype(jnp.bfloat16)
    selector = selector.reshape(offset_count, box_count * box_count)

    def translate(target_first, source_first, source_block):
        source_count = source_block.shape[3]
        pair_map = lax.dynamic_slice(
            tile_map, (target_first, source_first), (target_block, source_count)
        )
        pair_far = lax.dynamic_slice(
            far_mask, (target_first, source_first), (target_block, source_count)
        )
        pair_index = jnp.where(pair_far == 1, pair_map, tile_count)
        pair_rows = jnp.take(row_table, pair_index.reshape(-1), axis=2)
        expanded = jnp.dot(
            pair_rows.reshape(-1, offset_count), selector, preferred_element_type=jnp.float32
        )
        coupling = expanded.astype(jnp.bfloat16).reshape(
            2, directions_here, target_block, source_count, box_count, box_count
        )
        values = source_block.reshape(directions_here, 2 * illum_here, source_count, box_count)
        combos = jnp.einsum(
            "klcy,qkacxy->klqax", values, coupling, preferred_element_type=jnp.float32
        )
        combos = combos.reshape(directions_here, 2, illum_here, 2, target_block * box_count)
        incoming_real = combos[:, 0, :, 0] - combos[:, 1, :, 1]
        incoming_imag = combos[:, 1, :, 0] + combos[:, 0, :, 1]
        return jnp.stack([incoming_real, incoming_imag], axis=1)

    slab_first = lax.axis_index("slab") * own_rows

    def block_rows(block_index):
        return translate(block_index * target_block, slab_first, outgoing)

    summed = lax.psum_scatter(
        lax.map(block_rows, jnp.arange(block_count * lax.axis_size("slab"), dtype=jnp.int32)),
        "slab",
        scatter_dimension=0,
        tiled=True,
    )
    incoming = summed.astype(jnp.bfloat16)
    incoming = incoming.reshape(incoming.shape[:4] + (target_block, box_count))
    item_rows = lax.all_to_all(incoming, "wide", split_axis=5, concat_axis=1, tiled=True)

    def product(left_side, right_side):
        return jnp.einsum(
            "bkrax,pk->baxrp", left_side, right_side, preferred_element_type=jnp.float32
        )

    items_real = item_rows[:, :, 0]
    items_imag = item_rows[:, :, 1]
    field_real = product(items_real, disaggregation[0]) - product(items_imag, disaggregation[1])
    field_imag = product(items_real, disaggregation[1]) + product(items_imag, disaggregation[0])
    stacked = jnp.stack([field_real, field_imag], axis=3).astype(jnp.bfloat16)
    return stacked.reshape((stacked.shape[0] * stacked.shape[1],) + stacked.shape[2:])


def local(wide, slab, sub, *args):
    source, aggregation, translators, _, _, box_offsets, _ = args
    rows, columns, _, illum, unknowns = source.shape
    share = aggregation.shape[1] // (wide * slab * sub)
    tiles = (
        2 * rows * columns == LANES
        and 2 * box_offsets.shape[0] == LANES
        and columns * wide == box_offsets.shape[0]
        and slab == 2
        and wide == 4
        and columns == 16
        and illum == 16
        and share % 32 == 0
        and unknowns == LANES
        and LANES < translators.shape[3] <= 2 * LANES
        and translators.shape[2] <= 32
    )
    if tiles:
        return tiled_local(wide, slab, sub, *args)
    return general_local(*args)


def solution(mesh):
    placed = (
        P(("groups", "slab"), "wide", None, "sub", None),
        P(None, "groups", None),
        P(None, ("groups", "wide"), None, None),
        P(),
        P(),
        P(),
        P(None, None, "groups"),
    )
    return jax.shard_map(
        functools.partial(local, mesh.shape["wide"], mesh.shape["slab"], mesh.shape["sub"]),
        mesh=mesh,
        in_specs=placed,
        out_specs=P(("groups", "slab"), "wide", None, "sub", None),
        check_vma=False,
    )
```

```python
import functools

import jax
import jax.numpy as jnp
from jax import lax
from jax.experimental import pallas as pl
from jax.experimental.pallas import tpu as pltpu
from jax.sharding import PartitionSpec as P

OWNERS = ("wide", "slab", "sub")
LANES = 128
MIB = 1024 * 1024
PITCH = 36
SPARE = 40
NT = (((1,), (1,)), ((), ()))
TN = (((0,), (0,)), ((), ()))


def outgoing_kernel(boxes, illum, devices, half, place_ref, src_ref, agg_ref, out_ref, wide_src, wide_out):
    unknowns = src_ref.shape[1]
    wide_src[0:src_ref.shape[0]] = src_ref[...].astype(jnp.float32)
    real = agg_ref[0].astype(jnp.float32)
    imag = agg_ref[1].astype(jnp.float32)

    def pick(array, part):
        return jnp.concatenate(
            [array[(2 * d + part) * half:(2 * d + part + 1) * half] for d in range(devices)], axis=0
        )

    real_low, real_high = pick(real, 0), pick(real, 1)
    imag_low, imag_high = pick(imag, 0), pick(imag, 1)
    to_real = jnp.concatenate([real_low, -imag_low, real_high, -imag_high], axis=1).astype(jnp.bfloat16)
    to_imag = jnp.concatenate([imag_low, real_low, imag_high, real_high], axis=1).astype(jnp.bfloat16)
    zeros = jnp.zeros((boxes, 2 * unknowns), jnp.bfloat16)
    rows = devices * half
    for r in range(illum):
        both = jnp.concatenate(
            [wide_src[pl.ds(q * illum + r, boxes, stride=2 * illum), :] for q in range(2)], axis=1
        ).astype(jnp.bfloat16)
        right = jnp.concatenate(
            [jnp.concatenate([both, zeros], axis=1), jnp.concatenate([zeros, both], axis=1)], axis=0
        )
        for q, left in ((0, to_real), (1, to_imag)):
            wide_out[pl.ds(q * illum + r, rows, stride=PITCH), :] = lax.dot_general(
                left, right, NT, preferred_element_type=jnp.float32
            )
    tall = 2 * illum
    for g in range(rows):
        out_ref[g * tall:(g + 1) * tall] = wide_out[g * PITCH:g * PITCH + tall].astype(jnp.bfloat16)


def expand_kernel(middle, base_ref, index_ref, table_ref, out_ref, choice, left, wide):
    batch, translators, offsets = table_ref.shape[1:]
    depth = out_ref.shape[3]
    tall = 2 * depth
    rows = 2 * batch * tall

    @pl.when(pl.program_id(0) == 0)
    def _():
        offset = lax.broadcasted_iota(jnp.int32, (2 * LANES, LANES), 0)
        for x in range(tall):
            choice[:, x * LANES:(x + 1) * LANES] = jnp.where(
                offset == index_ref[x:x + 1, :], 1.0, 0.0
            ).astype(jnp.bfloat16)
        left[...] = jnp.zeros_like(left)

    for q in range(2):
        for k in range(batch):
            row = (q * batch + k) * tall
            left[row:row + translators, 0:offsets] = table_ref[q, k]
    table = left[...]
    for x in range(0, tall, 2):
        picked = jnp.dot(
            table, choice[:, x * LANES:(x + 2) * LANES], preferred_element_type=jnp.float32
        )
        wide[pl.ds(x, rows, stride=PITCH), :] = picked[:, :LANES]
        wide[pl.ds(x + 1, rows, stride=PITCH), :] = picked[:, LANES:]
    for k in range(batch):
        for v in range(2):
            out_ref[v, k, middle] = jnp.zeros(out_ref.shape[3:], jnp.bfloat16)
        for t in range(translators):
            if abs(t - middle) < 2:
                continue
            for q in range(2):
                row = ((q * batch + k) * tall + t) * PITCH
                for v in range(2):
                    out_ref[v, k, t, :, q * LANES:(q + 1) * LANES] = wide[
                        row + v * depth:row + (v + 1) * depth
                    ].astype(jnp.bfloat16)


def translate_kernel(wide, slab, sub, rows, columns, pair_ref, own_ref, far_ref, low_ref, high_ref, out_ref):
    illum = own_ref.shape[3]
    steps = low_ref.shape[1]
    all_rows = slab * rows
    lane = lax.broadcasted_iota(jnp.int32, (illum, LANES), 1)
    group = lane // columns
    groups = LANES // columns
    lower = lane < LANES // 2
    zero = jnp.zeros((illum, LANES), jnp.bfloat16)
    for step in range(steps):
        here = step
        sums = [None, None]
        turned = {}

        def turn(s, u, q, w, amount):
            key = (s, u, q, w, amount)
            if key not in turned:
                tile = (own_ref, far_ref)[w // 2][(w % 2 * slab + s) * sub + u, here, q]
                turned[key] = pltpu.roll(tile, amount * columns, 1) if amount else tile
            return turned[key]

        for c in range(all_rows):
            s, own = c // rows, c % rows
            for k2 in range(2):
                position = k2 * rows + own
                parts = {}
                for u in range(sub):
                    for q in range(2):
                        for h in range(2):
                            tile = zero
                            for w in range(wide):
                                place = h * wide + w
                                tile = jnp.where(
                                    group == place,
                                    turn(s, u, q, w, (place - position) % groups),
                                    tile,
                                )
                            parts[u, q, h] = tile
                left = []
                for h in range(2):
                    for u in range(sub):
                        left.append(jnp.concatenate([parts[u, 0, h], -parts[u, 1, h]], axis=1))
                        left.append(jnp.concatenate([parts[u, 1, h], parts[u, 0, h]], axis=1))
                left = jnp.concatenate(left, axis=0)
                right = jnp.concatenate(
                    [
                        (low_ref, high_ref)[k2][0, step, pair_ref[a * all_rows + c]]
                        for a in range(all_rows)
                    ],
                    axis=0,
                )
                product = lax.dot_general(left, right, NT, preferred_element_type=jnp.float32)
                sums[k2] = product if sums[k2] is None else sums[k2] + product
        for h in range(2):
            for u in range(sub):
                for q in range(2):
                    row = ((h * sub + u) * 2 + q) * illum
                    first = sums[0][row:row + illum]
                    second = sums[1][row:row + illum]
                    for s in range(slab):
                        if s == 0:
                            tile = jnp.where(lower, first, pltpu.roll(second, LANES // 2, 1))
                        else:
                            tile = jnp.where(lower, pltpu.roll(first, LANES // 2, 1), second)
                        out_ref[(h * slab + s) * sub + u, here, q] = tile.astype(jnp.bfloat16)


def pattern_kernel(devices, half, place_ref, dis_ref, out_ref):
    real = dis_ref[0].astype(jnp.float32).T
    imag = dis_ref[1].astype(jnp.float32).T

    def pick(array, part):
        return jnp.concatenate(
            [array[(2 * d + part) * half:(2 * d + part + 1) * half] for d in range(devices)], axis=0
        )

    sides = []
    for part in range(2):
        real_part, imag_part = pick(real, part), pick(imag, part)
        sides.append(
            jnp.concatenate(
                [
                    jnp.concatenate([real_part, imag_part], axis=1),
                    jnp.concatenate([-imag_part, real_part], axis=1),
                ],
                axis=0,
            )
        )
    out_ref[...] = jnp.concatenate(sides, axis=1).astype(jnp.bfloat16)


def field_kernel(boxes, illum, inc_ref, pattern_ref, out_ref, wide_inc, wide_out):
    unknowns = out_ref.shape[1]
    tall = 2 * illum
    rows = inc_ref.shape[0] // tall
    for g in range(rows):
        wide_inc[g * PITCH:g * PITCH + tall] = inc_ref[g * tall:(g + 1) * tall].astype(jnp.float32)
    right = pattern_ref[...]
    for r in range(illum):
        left = jnp.concatenate(
            [wide_inc[pl.ds(q * illum + r, rows, stride=PITCH), :] for q in range(2)], axis=0
        ).astype(jnp.bfloat16)
        product = lax.dot_general(left, right, TN, preferred_element_type=jnp.float32)
        total = product[:boxes, :2 * unknowns] + product[boxes:, 2 * unknowns:]
        for q in range(2):
            wide_out[pl.ds(q * illum + r, boxes, stride=PITCH), :] = total[
                :, q * unknowns:(q + 1) * unknowns
            ]
    for g in range(boxes):
        out_ref[g * tall:(g + 1) * tall] = wide_out[g * PITCH:g * PITCH + tall].astype(out_ref.dtype)


def tiled_local(wide, slab, sub, source, aggregation, translators, tile_map, far_mask, box_offsets, disaggregation):
    rows, columns, _, illum, unknowns = source.shape
    devices = wide * slab * sub
    directions = aggregation.shape[1]
    half = directions // devices // 2
    boxes = rows * columns
    all_rows = slab * rows
    count = translators.shape[2]
    offsets = translators.shape[3]
    middle = count // 2

    near = devices // 2
    lines = near * half * 2 * illum
    block = (near, half, 2, illum, LANES)
    shape = (boxes * 2 * illum, unknowns)
    place = lax.axis_index("wide") // 2
    neighbours = [[first * near + d for d in range(near)] for first in range(2)]

    def exchange(values):
        return lax.all_to_all(
            values, OWNERS, split_axis=0, concat_axis=0, tiled=True, axis_index_groups=neighbours
        )

    def cross(values):
        return lax.ppermute(values, "wide", [(w, (w + wide // 2) % wide) for w in range(wide)])

    def outgoing(values, limit):
        return pl.pallas_call(
            functools.partial(outgoing_kernel, boxes, illum, near, half),
            grid_spec=pltpu.PrefetchScalarGridSpec(
                num_scalar_prefetch=1,
                grid=(1,),
                in_specs=[
                    pl.BlockSpec(shape, lambda i, place: (0, 0)),
                    pl.BlockSpec((2, directions // 2, unknowns), lambda i, place: (0, place[0], 0)),
                ],
                out_specs=pl.BlockSpec((lines, LANES), lambda i, place: (0, 0)),
                scratch_shapes=[
                    pltpu.VMEM((shape[0] + SPARE, unknowns), jnp.float32),
                    pltpu.VMEM((near * half * PITCH + SPARE, LANES), jnp.float32),
                ],
            ),
            out_shape=jax.ShapeDtypeStruct((lines, LANES), jnp.bfloat16),
            compiler_params=pltpu.CompilerParams(vmem_limit_bytes=limit * MIB),
            name="outgoing",
        )(place.reshape(1), values, aggregation).reshape(block)

    flat = source.reshape(shape)
    across_source = cross(flat)
    own = exchange(outgoing(flat, 56))

    side = box_offsets.shape[0]
    x_half = side // 2
    by_side = jnp.roll(box_offsets, x_half, axis=0)
    by_side = jnp.where(place == 0, by_side, jnp.roll(box_offsets, x_half, axis=1))
    by_side = by_side.reshape(2, 2, columns, side)
    index = jnp.concatenate([by_side[:, 0], by_side[:, 1]], axis=-1).reshape(x_half, 2 * side)
    base = lax.axis_index("slab") * sub + lax.axis_index("sub")
    pattern = pl.pallas_call(
        functools.partial(pattern_kernel, near, half),
        grid_spec=pltpu.PrefetchScalarGridSpec(
            num_scalar_prefetch=1,
            grid=(1,),
            in_specs=[pl.BlockSpec((2, unknowns, directions // 2), lambda i, place: (0, 0, place[0]))],
            out_specs=pl.BlockSpec((2 * near * half, 4 * unknowns), lambda i, place: (0, 0)),
        ),
        out_shape=jax.ShapeDtypeStruct((2 * near * half, 4 * unknowns), jnp.bfloat16),
        compiler_params=pltpu.CompilerParams(vmem_limit_bytes=8 * MIB),
        name="pattern",
    )(place.reshape(1), disaggregation)
    base = lax.axis_index("slab") * sub + lax.axis_index("sub")
    batch = 8

    def expand(k2):
        per_part = half // batch
        return pl.pallas_call(
            functools.partial(expand_kernel, middle),
            grid_spec=pltpu.PrefetchScalarGridSpec(
                num_scalar_prefetch=1,
                grid=(per_part,),
                in_specs=[
                    pl.BlockSpec((x_half, 2 * side), lambda k, base: (0, 0)),
                    pl.BlockSpec(
                        (2, batch, count, offsets),
                        lambda k, base: (0, (2 * base[0] + k2) * per_part + k, 0, 0),
                    ),
                ],
                out_specs=pl.BlockSpec(
                    (2, batch, count, columns, 2 * LANES), lambda k, base: (0, k, 0, 0, 0)
                ),
                scratch_shapes=[
                    pltpu.VMEM((2 * LANES, x_half * LANES), jnp.bfloat16),
                    pltpu.VMEM((2 * batch * x_half, 2 * LANES), jnp.bfloat16),
                    pltpu.VMEM((2 * batch * x_half * PITCH + SPARE, LANES), jnp.float32),
                ],
            ),
            out_shape=jax.ShapeDtypeStruct((2, half, count, columns, 2 * LANES), jnp.bfloat16),
            compiler_params=pltpu.CompilerParams(vmem_limit_bytes=56 * MIB),
            cost_estimate=pl.CostEstimate(
                flops=8 * 2 * 2 * half * x_half * 2 * LANES * x_half * LANES,
                bytes_accessed=8 * 2 * half * count * columns * 2 * LANES * 2,
                transcendentals=0,
            ),
            name="expand",
        )(base.reshape(1), index, translators)

    first = expand(0)
    across_source, first, pattern = lax.optimization_barrier((across_source, first, pattern))
    received = own, exchange(outgoing(across_source, 16))
    expanded = first, expand(1)
    pairs = jnp.where(far_mask == 1, tile_map, middle).reshape(-1)
    steps = 4
    part = (near, steps) + block[2:]

    def translate(v):
        return pl.pallas_call(
            functools.partial(translate_kernel, wide, slab, sub, rows, columns),
            grid_spec=pltpu.PrefetchScalarGridSpec(
                num_scalar_prefetch=1,
                grid=(half // steps,),
                in_specs=[
                    pl.BlockSpec(part, lambda k, pairs: (0, k, 0, 0, 0)),
                    pl.BlockSpec(part, lambda k, pairs: (0, k, 0, 0, 0)),
                    pl.BlockSpec(
                        (1, steps, count, columns, 2 * LANES), lambda k, pairs: (v, k, 0, 0, 0)
                    ),
                    pl.BlockSpec(
                        (1, steps, count, columns, 2 * LANES), lambda k, pairs: (v, k, 0, 0, 0)
                    ),
                ],
                out_specs=pl.BlockSpec(part, lambda k, pairs: (0, k, 0, 0, 0)),
            ),
            out_shape=jax.ShapeDtypeStruct(block, jnp.bfloat16),
            compiler_params=pltpu.CompilerParams(vmem_limit_bytes=50 * MIB),
            name="translate",
        )(pairs, *received, *expanded)

    def field(values, kind):
        return pl.pallas_call(
            functools.partial(field_kernel, boxes, illum),
            out_shape=jax.ShapeDtypeStruct(shape, kind),
            scratch_shapes=[
                pltpu.VMEM((near * half * PITCH + SPARE, LANES), jnp.float32),
                pltpu.VMEM((boxes * PITCH + SPARE, unknowns), jnp.float32),
            ],
            compiler_params=pltpu.CompilerParams(vmem_limit_bytes=12 * MIB),
            name="field",
        )(values.reshape(lines, LANES), pattern)

    far_half = exchange(translate(0))
    near_half = exchange(translate(1))
    across = cross(field(far_half, jnp.bfloat16))
    total = field(near_half, jnp.float32) + across.astype(jnp.float32)
    return total.astype(jnp.bfloat16).reshape(source.shape)


def aggregate(values, pattern_real, pattern_imag):

    def product(left_side, right_side):
        return jnp.einsum(
            "axrp,kp->krax", left_side, right_side, preferred_element_type=jnp.float32
        )

    values_real = values[:, :, 0]
    values_imag = values[:, :, 1]
    out_real = product(values_real, pattern_real) - product(values_imag, pattern_imag)
    out_imag = product(values_real, pattern_imag) + product(values_imag, pattern_real)
    return jnp.stack([out_real, out_imag], axis=1).astype(jnp.bfloat16)


def general_local(source, aggregation, translators, tile_map, far_mask, box_offsets, disaggregation):
    own_rows = source.shape[0]
    tile_count = translators.shape[2]
    offset_count = translators.shape[3]
    box_count = box_offsets.shape[0]
    target_block = 2
    block_count = own_rows // target_block
    outgoing = lax.all_to_all(
        aggregate(source, aggregation[0], aggregation[1]),
        "wide",
        split_axis=0,
        concat_axis=4,
        tiled=True,
    )
    directions_here = outgoing.shape[0]
    illum_here = outgoing.shape[2]
    row_table = jnp.concatenate(
        [translators, jnp.zeros((2, directions_here, 1, offset_count), jnp.bfloat16)], axis=2
    )
    offset_ids = lax.broadcasted_iota(jnp.int32, (offset_count, box_count, box_count), 0)
    selector = (offset_ids == box_offsets[None, :, :]).astype(jnp.bfloat16)
    selector = selector.reshape(offset_count, box_count * box_count)

    def translate(target_first, source_first, source_block):
        source_count = source_block.shape[3]
        pair_map = lax.dynamic_slice(
            tile_map, (target_first, source_first), (target_block, source_count)
        )
        pair_far = lax.dynamic_slice(
            far_mask, (target_first, source_first), (target_block, source_count)
        )
        pair_index = jnp.where(pair_far == 1, pair_map, tile_count)
        pair_rows = jnp.take(row_table, pair_index.reshape(-1), axis=2)
        expanded = jnp.dot(
            pair_rows.reshape(-1, offset_count), selector, preferred_element_type=jnp.float32
        )
        coupling = expanded.astype(jnp.bfloat16).reshape(
            2, directions_here, target_block, source_count, box_count, box_count
        )
        values = source_block.reshape(directions_here, 2 * illum_here, source_count, box_count)
        combos = jnp.einsum(
            "klcy,qkacxy->klqax", values, coupling, preferred_element_type=jnp.float32
        )
        combos = combos.reshape(directions_here, 2, illum_here, 2, target_block * box_count)
        incoming_real = combos[:, 0, :, 0] - combos[:, 1, :, 1]
        incoming_imag = combos[:, 1, :, 0] + combos[:, 0, :, 1]
        return jnp.stack([incoming_real, incoming_imag], axis=1)

    slab_first = lax.axis_index("slab") * own_rows

    def block_rows(block_index):
        return translate(block_index * target_block, slab_first, outgoing)

    summed = lax.psum_scatter(
        lax.map(block_rows, jnp.arange(block_count * lax.axis_size("slab"), dtype=jnp.int32)),
        "slab",
        scatter_dimension=0,
        tiled=True,
    )
    incoming = summed.astype(jnp.bfloat16)
    incoming = incoming.reshape(incoming.shape[:4] + (target_block, box_count))
    item_rows = lax.all_to_all(incoming, "wide", split_axis=5, concat_axis=1, tiled=True)

    def product(left_side, right_side):
        return jnp.einsum(
            "bkrax,pk->baxrp", left_side, right_side, preferred_element_type=jnp.float32
        )

    items_real = item_rows[:, :, 0]
    items_imag = item_rows[:, :, 1]
    field_real = product(items_real, disaggregation[0]) - product(items_imag, disaggregation[1])
    field_imag = product(items_real, disaggregation[1]) + product(items_imag, disaggregation[0])
    stacked = jnp.stack([field_real, field_imag], axis=3).astype(jnp.bfloat16)
    return stacked.reshape((stacked.shape[0] * stacked.shape[1],) + stacked.shape[2:])


def local(wide, slab, sub, *args):
    source, aggregation, translators, _, _, box_offsets, _ = args
    rows, columns, _, illum, unknowns = source.shape
    share = aggregation.shape[1] // (wide * slab * sub)
    tiles = (
        2 * rows * columns == LANES
        and 2 * box_offsets.shape[0] == LANES
        and columns * wide == box_offsets.shape[0]
        and slab == 2
        and wide == 4
        and columns == 16
        and illum == 16
        and share % 32 == 0
        and unknowns == LANES
        and LANES < translators.shape[3] <= 2 * LANES
        and translators.shape[2] <= 32
    )
    if tiles:
        return tiled_local(wide, slab, sub, *args)
    return general_local(*args)


def solution(mesh):
    placed = (
        P(("groups", "slab"), "wide", None, "sub", None),
        P(None, "groups", None),
        P(None, ("groups", "wide"), None, None),
        P(),
        P(),
        P(),
        P(None, None, "groups"),
    )
    return jax.shard_map(
        functools.partial(local, mesh.shape["wide"], mesh.shape["slab"], mesh.shape["sub"]),
        mesh=mesh,
        in_specs=placed,
        out_specs=P(("groups", "slab"), "wide", None, "sub", None),
        check_vma=False,
    )
```

```python
import functools

import jax
import jax.numpy as jnp
from jax import lax
from jax.experimental import pallas as pl
from jax.experimental.pallas import tpu as pltpu
from jax.sharding import PartitionSpec as P

OWNERS = ("wide", "slab", "sub")
LANES = 128
MIB = 1024 * 1024
PITCH = 36
SPARE = 40
NT = (((1,), (1,)), ((), ()))
TN = (((0,), (0,)), ((), ()))


def outgoing_kernel(boxes, illum, devices, half, place_ref, src_ref, agg_ref, out_ref, wide_src, wide_out):
    unknowns = src_ref.shape[1]
    wide_src[0:src_ref.shape[0]] = src_ref[...].astype(jnp.float32)
    real = agg_ref[0].astype(jnp.float32)
    imag = agg_ref[1].astype(jnp.float32)

    def pick(array, part):
        return jnp.concatenate(
            [array[(2 * d + part) * half:(2 * d + part + 1) * half] for d in range(devices)], axis=0
        )

    real_low, real_high = pick(real, 0), pick(real, 1)
    imag_low, imag_high = pick(imag, 0), pick(imag, 1)
    to_real = jnp.concatenate([real_low, -imag_low, real_high, -imag_high], axis=1).astype(jnp.bfloat16)
    to_imag = jnp.concatenate([imag_low, real_low, imag_high, real_high], axis=1).astype(jnp.bfloat16)
    zeros = jnp.zeros((boxes, 2 * unknowns), jnp.bfloat16)
    rows = devices * half
    for r in range(illum):
        both = jnp.concatenate(
            [wide_src[pl.ds(q * illum + r, boxes, stride=2 * illum), :] for q in range(2)], axis=1
        ).astype(jnp.bfloat16)
        right = jnp.concatenate(
            [jnp.concatenate([both, zeros], axis=1), jnp.concatenate([zeros, both], axis=1)], axis=0
        )
        for q, left in ((0, to_real), (1, to_imag)):
            wide_out[pl.ds(q * illum + r, rows, stride=PITCH), :] = lax.dot_general(
                left, right, NT, preferred_element_type=jnp.float32
            )
    tall = 2 * illum
    for g in range(rows):
        out_ref[g * tall:(g + 1) * tall] = wide_out[g * PITCH:g * PITCH + tall].astype(jnp.bfloat16)


def expand_kernel(middle, base_ref, index_ref, table_ref, out_ref, choice, left, wide):
    batch, translators, offsets = table_ref.shape[1:]
    depth = out_ref.shape[3]
    tall = 2 * depth
    rows = 2 * batch * tall

    @pl.when(pl.program_id(0) == 0)
    def _():
        offset = lax.broadcasted_iota(jnp.int32, (2 * LANES, LANES), 0)
        for x in range(tall):
            choice[:, x * LANES:(x + 1) * LANES] = jnp.where(
                offset == index_ref[x:x + 1, :], 1.0, 0.0
            ).astype(jnp.bfloat16)
        left[...] = jnp.zeros_like(left)

    for q in range(2):
        for k in range(batch):
            row = (q * batch + k) * tall
            left[row:row + translators, 0:offsets] = table_ref[q, k]
    table = left[...]
    for x in range(0, tall, 2):
        picked = jnp.dot(
            table, choice[:, x * LANES:(x + 2) * LANES], preferred_element_type=jnp.float32
        )
        wide[pl.ds(x, rows, stride=PITCH), :] = picked[:, :LANES]
        wide[pl.ds(x + 1, rows, stride=PITCH), :] = picked[:, LANES:]
    for k in range(batch):
        for v in range(2):
            out_ref[v, k, middle - 1] = jnp.zeros(out_ref.shape[3:], jnp.bfloat16)
        for t in range(translators):
            if abs(t - middle) < 2:
                continue
            for q in range(2):
                row = ((q * batch + k) * tall + t) * PITCH
                for v in range(2):
                    out_ref[v, k, t if t < middle else t - 2, :, q * LANES:(q + 1) * LANES] = wide[
                        row + v * depth:row + (v + 1) * depth
                    ].astype(jnp.bfloat16)


def translate_kernel(wide, slab, sub, rows, columns, pair_ref, own_ref, far_ref, low_ref, high_ref, out_ref):
    illum = own_ref.shape[3]
    steps = low_ref.shape[1]
    all_rows = slab * rows
    lane = lax.broadcasted_iota(jnp.int32, (illum, LANES), 1)
    group = lane // columns
    groups = LANES // columns
    lower = lane < LANES // 2
    zero = jnp.zeros((illum, LANES), jnp.bfloat16)
    for step in range(steps):
        here = step
        sums = [None, None]
        turned = {}

        def turn(s, u, q, w, amount):
            key = (s, u, q, w, amount)
            if key not in turned:
                tile = (own_ref, far_ref)[w // 2][(w % 2 * slab + s) * sub + u, here, q]
                turned[key] = pltpu.roll(tile, amount * columns, 1) if amount else tile
            return turned[key]

        for c in range(all_rows):
            s, own = c // rows, c % rows
            for k2 in range(2):
                position = k2 * rows + own
                parts = {}
                for u in range(sub):
                    for q in range(2):
                        for h in range(2):
                            tile = zero
                            for w in range(wide):
                                place = h * wide + w
                                tile = jnp.where(
                                    group == place,
                                    turn(s, u, q, w, (place - position) % groups),
                                    tile,
                                )
                            parts[u, q, h] = tile
                left = []
                for h in range(2):
                    for u in range(sub):
                        left.append(jnp.concatenate([parts[u, 0, h], -parts[u, 1, h]], axis=1))
                        left.append(jnp.concatenate([parts[u, 1, h], parts[u, 0, h]], axis=1))
                left = jnp.concatenate(left, axis=0)
                right = jnp.concatenate(
                    [
                        (low_ref, high_ref)[k2][0, step, pair_ref[a * all_rows + c]]
                        for a in range(all_rows)
                    ],
                    axis=0,
                )
                product = lax.dot_general(left, right, NT, preferred_element_type=jnp.float32)
                sums[k2] = product if sums[k2] is None else sums[k2] + product
        for h in range(2):
            for u in range(sub):
                for q in range(2):
                    row = ((h * sub + u) * 2 + q) * illum
                    first = sums[0][row:row + illum]
                    second = sums[1][row:row + illum]
                    for s in range(slab):
                        if s == 0:
                            tile = jnp.where(lower, first, pltpu.roll(second, LANES // 2, 1))
                        else:
                            tile = jnp.where(lower, pltpu.roll(first, LANES // 2, 1), second)
                        out_ref[(h * slab + s) * sub + u, here, q] = tile.astype(jnp.bfloat16)


def pattern_kernel(devices, half, place_ref, dis_ref, out_ref):
    real = dis_ref[0].astype(jnp.float32).T
    imag = dis_ref[1].astype(jnp.float32).T

    def pick(array, part):
        return jnp.concatenate(
            [array[(2 * d + part) * half:(2 * d + part + 1) * half] for d in range(devices)], axis=0
        )

    sides = []
    for part in range(2):
        real_part, imag_part = pick(real, part), pick(imag, part)
        sides.append(
            jnp.concatenate(
                [
                    jnp.concatenate([real_part, imag_part], axis=1),
                    jnp.concatenate([-imag_part, real_part], axis=1),
                ],
                axis=0,
            )
        )
    out_ref[...] = jnp.concatenate(sides, axis=1).astype(jnp.bfloat16)


def field_kernel(boxes, illum, inc_ref, pattern_ref, out_ref, wide_inc, wide_out):
    unknowns = out_ref.shape[1]
    tall = 2 * illum
    rows = inc_ref.shape[0] // tall
    for g in range(rows):
        wide_inc[g * PITCH:g * PITCH + tall] = inc_ref[g * tall:(g + 1) * tall].astype(jnp.float32)
    right = pattern_ref[...]
    for r in range(illum):
        left = jnp.concatenate(
            [wide_inc[pl.ds(q * illum + r, rows, stride=PITCH), :] for q in range(2)], axis=0
        ).astype(jnp.bfloat16)
        product = lax.dot_general(left, right, TN, preferred_element_type=jnp.float32)
        total = product[:boxes, :2 * unknowns] + product[boxes:, 2 * unknowns:]
        for q in range(2):
            wide_out[pl.ds(q * illum + r, boxes, stride=PITCH), :] = total[
                :, q * unknowns:(q + 1) * unknowns
            ]
    for g in range(boxes):
        out_ref[g * tall:(g + 1) * tall] = wide_out[g * PITCH:g * PITCH + tall].astype(out_ref.dtype)


def tiled_local(wide, slab, sub, source, aggregation, translators, tile_map, far_mask, box_offsets, disaggregation):
    rows, columns, _, illum, unknowns = source.shape
    devices = wide * slab * sub
    directions = aggregation.shape[1]
    half = directions // devices // 2
    boxes = rows * columns
    all_rows = slab * rows
    count = translators.shape[2]
    offsets = translators.shape[3]
    middle = count // 2

    near = devices // 2
    lines = near * half * 2 * illum
    block = (near, half, 2, illum, LANES)
    shape = (boxes * 2 * illum, unknowns)
    place = lax.axis_index("wide") // 2
    neighbours = [[first * near + d for d in range(near)] for first in range(2)]

    def exchange(values):
        return lax.all_to_all(
            values, OWNERS, split_axis=0, concat_axis=0, tiled=True, axis_index_groups=neighbours
        )

    def cross(values):
        return lax.ppermute(values, "wide", [(w, (w + wide // 2) % wide) for w in range(wide)])

    def outgoing(values, limit):
        return pl.pallas_call(
            functools.partial(outgoing_kernel, boxes, illum, near, half),
            grid_spec=pltpu.PrefetchScalarGridSpec(
                num_scalar_prefetch=1,
                grid=(1,),
                in_specs=[
                    pl.BlockSpec(shape, lambda i, place: (0, 0)),
                    pl.BlockSpec((2, directions // 2, unknowns), lambda i, place: (0, place[0], 0)),
                ],
                out_specs=pl.BlockSpec((lines, LANES), lambda i, place: (0, 0)),
                scratch_shapes=[
                    pltpu.VMEM((shape[0] + SPARE, unknowns), jnp.float32),
                    pltpu.VMEM((near * half * PITCH + SPARE, LANES), jnp.float32),
                ],
            ),
            out_shape=jax.ShapeDtypeStruct((lines, LANES), jnp.bfloat16),
            compiler_params=pltpu.CompilerParams(vmem_limit_bytes=limit * MIB),
            name="outgoing",
        )(place.reshape(1), values, aggregation).reshape(block)

    flat = source.reshape(shape)
    across_source = cross(flat)
    own = exchange(outgoing(flat, 56))

    side = box_offsets.shape[0]
    x_half = side // 2
    by_side = jnp.roll(box_offsets, x_half, axis=0)
    by_side = jnp.where(place == 0, by_side, jnp.roll(box_offsets, x_half, axis=1))
    by_side = by_side.reshape(2, 2, columns, side)
    index = jnp.concatenate([by_side[:, 0], by_side[:, 1]], axis=-1).reshape(x_half, 2 * side)
    base = lax.axis_index("slab") * sub + lax.axis_index("sub")
    pattern = pl.pallas_call(
        functools.partial(pattern_kernel, near, half),
        grid_spec=pltpu.PrefetchScalarGridSpec(
            num_scalar_prefetch=1,
            grid=(1,),
            in_specs=[pl.BlockSpec((2, unknowns, directions // 2), lambda i, place: (0, 0, place[0]))],
            out_specs=pl.BlockSpec((2 * near * half, 4 * unknowns), lambda i, place: (0, 0)),
        ),
        out_shape=jax.ShapeDtypeStruct((2 * near * half, 4 * unknowns), jnp.bfloat16),
        compiler_params=pltpu.CompilerParams(vmem_limit_bytes=8 * MIB),
        name="pattern",
    )(place.reshape(1), disaggregation)
    base = lax.axis_index("slab") * sub + lax.axis_index("sub")
    batch = 8

    def expand(k2):
        per_part = half // batch
        return pl.pallas_call(
            functools.partial(expand_kernel, middle),
            grid_spec=pltpu.PrefetchScalarGridSpec(
                num_scalar_prefetch=1,
                grid=(per_part,),
                in_specs=[
                    pl.BlockSpec((x_half, 2 * side), lambda k, base: (0, 0)),
                    pl.BlockSpec(
                        (2, batch, count, offsets),
                        lambda k, base: (0, (2 * base[0] + k2) * per_part + k, 0, 0),
                    ),
                ],
                out_specs=pl.BlockSpec(
                    (2, batch, count - 2, columns, 2 * LANES), lambda k, base: (0, k, 0, 0, 0)
                ),
                scratch_shapes=[
                    pltpu.VMEM((2 * LANES, x_half * LANES), jnp.bfloat16),
                    pltpu.VMEM((2 * batch * x_half, 2 * LANES), jnp.bfloat16),
                    pltpu.VMEM((2 * batch * x_half * PITCH + SPARE, LANES), jnp.float32),
                ],
            ),
            out_shape=jax.ShapeDtypeStruct((2, half, count - 2, columns, 2 * LANES), jnp.bfloat16),
            compiler_params=pltpu.CompilerParams(vmem_limit_bytes=56 * MIB),
            cost_estimate=pl.CostEstimate(
                flops=8 * 2 * 2 * half * x_half * 2 * LANES * x_half * LANES,
                bytes_accessed=8 * 2 * half * count * columns * 2 * LANES * 2,
                transcendentals=0,
            ),
            name="expand",
        )(base.reshape(1), index, translators)

    first = expand(0)
    across_source, first, pattern = lax.optimization_barrier((across_source, first, pattern))
    received = own, exchange(outgoing(across_source, 16))
    expanded = first, expand(1)
    slots = jnp.where(tile_map < middle, tile_map, tile_map - 2)
    pairs = jnp.where(far_mask == 1, slots, middle - 1).reshape(-1)
    steps = 4
    part = (near, steps) + block[2:]

    def translate(v):
        return pl.pallas_call(
            functools.partial(translate_kernel, wide, slab, sub, rows, columns),
            grid_spec=pltpu.PrefetchScalarGridSpec(
                num_scalar_prefetch=1,
                grid=(half // steps,),
                in_specs=[
                    pl.BlockSpec(part, lambda k, pairs: (0, k, 0, 0, 0)),
                    pl.BlockSpec(part, lambda k, pairs: (0, k, 0, 0, 0)),
                    pl.BlockSpec(
                        (1, steps, count - 2, columns, 2 * LANES), lambda k, pairs: (v, k, 0, 0, 0)
                    ),
                    pl.BlockSpec(
                        (1, steps, count - 2, columns, 2 * LANES), lambda k, pairs: (v, k, 0, 0, 0)
                    ),
                ],
                out_specs=pl.BlockSpec(part, lambda k, pairs: (0, k, 0, 0, 0)),
            ),
            out_shape=jax.ShapeDtypeStruct(block, jnp.bfloat16),
            compiler_params=pltpu.CompilerParams(vmem_limit_bytes=50 * MIB),
            name="translate",
        )(pairs, *received, *expanded)

    def field(values, kind):
        return pl.pallas_call(
            functools.partial(field_kernel, boxes, illum),
            out_shape=jax.ShapeDtypeStruct(shape, kind),
            scratch_shapes=[
                pltpu.VMEM((near * half * PITCH + SPARE, LANES), jnp.float32),
                pltpu.VMEM((boxes * PITCH + SPARE, unknowns), jnp.float32),
            ],
            compiler_params=pltpu.CompilerParams(vmem_limit_bytes=12 * MIB),
            name="field",
        )(values.reshape(lines, LANES), pattern)

    far_half = exchange(translate(0))
    near_half = exchange(translate(1))
    across = cross(field(far_half, jnp.bfloat16))
    total = field(near_half, jnp.float32) + across.astype(jnp.float32)
    return total.astype(jnp.bfloat16).reshape(source.shape)


def aggregate(values, pattern_real, pattern_imag):

    def product(left_side, right_side):
        return jnp.einsum(
            "axrp,kp->krax", left_side, right_side, preferred_element_type=jnp.float32
        )

    values_real = values[:, :, 0]
    values_imag = values[:, :, 1]
    out_real = product(values_real, pattern_real) - product(values_imag, pattern_imag)
    out_imag = product(values_real, pattern_imag) + product(values_imag, pattern_real)
    return jnp.stack([out_real, out_imag], axis=1).astype(jnp.bfloat16)


def general_local(source, aggregation, translators, tile_map, far_mask, box_offsets, disaggregation):
    own_rows = source.shape[0]
    tile_count = translators.shape[2]
    offset_count = translators.shape[3]
    box_count = box_offsets.shape[0]
    target_block = 2
    block_count = own_rows // target_block
    outgoing = lax.all_to_all(
        aggregate(source, aggregation[0], aggregation[1]),
        "wide",
        split_axis=0,
        concat_axis=4,
        tiled=True,
    )
    directions_here = outgoing.shape[0]
    illum_here = outgoing.shape[2]
    row_table = jnp.concatenate(
        [translators, jnp.zeros((2, directions_here, 1, offset_count), jnp.bfloat16)], axis=2
    )
    offset_ids = lax.broadcasted_iota(jnp.int32, (offset_count, box_count, box_count), 0)
    selector = (offset_ids == box_offsets[None, :, :]).astype(jnp.bfloat16)
    selector = selector.reshape(offset_count, box_count * box_count)

    def translate(target_first, source_first, source_block):
        source_count = source_block.shape[3]
        pair_map = lax.dynamic_slice(
            tile_map, (target_first, source_first), (target_block, source_count)
        )
        pair_far = lax.dynamic_slice(
            far_mask, (target_first, source_first), (target_block, source_count)
        )
        pair_index = jnp.where(pair_far == 1, pair_map, tile_count)
        pair_rows = jnp.take(row_table, pair_index.reshape(-1), axis=2)
        expanded = jnp.dot(
            pair_rows.reshape(-1, offset_count), selector, preferred_element_type=jnp.float32
        )
        coupling = expanded.astype(jnp.bfloat16).reshape(
            2, directions_here, target_block, source_count, box_count, box_count
        )
        values = source_block.reshape(directions_here, 2 * illum_here, source_count, box_count)
        combos = jnp.einsum(
            "klcy,qkacxy->klqax", values, coupling, preferred_element_type=jnp.float32
        )
        combos = combos.reshape(directions_here, 2, illum_here, 2, target_block * box_count)
        incoming_real = combos[:, 0, :, 0] - combos[:, 1, :, 1]
        incoming_imag = combos[:, 1, :, 0] + combos[:, 0, :, 1]
        return jnp.stack([incoming_real, incoming_imag], axis=1)

    slab_first = lax.axis_index("slab") * own_rows

    def block_rows(block_index):
        return translate(block_index * target_block, slab_first, outgoing)

    summed = lax.psum_scatter(
        lax.map(block_rows, jnp.arange(block_count * lax.axis_size("slab"), dtype=jnp.int32)),
        "slab",
        scatter_dimension=0,
        tiled=True,
    )
    incoming = summed.astype(jnp.bfloat16)
    incoming = incoming.reshape(incoming.shape[:4] + (target_block, box_count))
    item_rows = lax.all_to_all(incoming, "wide", split_axis=5, concat_axis=1, tiled=True)

    def product(left_side, right_side):
        return jnp.einsum(
            "bkrax,pk->baxrp", left_side, right_side, preferred_element_type=jnp.float32
        )

    items_real = item_rows[:, :, 0]
    items_imag = item_rows[:, :, 1]
    field_real = product(items_real, disaggregation[0]) - product(items_imag, disaggregation[1])
    field_imag = product(items_real, disaggregation[1]) + product(items_imag, disaggregation[0])
    stacked = jnp.stack([field_real, field_imag], axis=3).astype(jnp.bfloat16)
    return stacked.reshape((stacked.shape[0] * stacked.shape[1],) + stacked.shape[2:])


def local(wide, slab, sub, *args):
    source, aggregation, translators, _, _, box_offsets, _ = args
    rows, columns, _, illum, unknowns = source.shape
    share = aggregation.shape[1] // (wide * slab * sub)
    tiles = (
        2 * rows * columns == LANES
        and 2 * box_offsets.shape[0] == LANES
        and columns * wide == box_offsets.shape[0]
        and slab == 2
        and wide == 4
        and columns == 16
        and illum == 16
        and share % 32 == 0
        and unknowns == LANES
        and LANES < translators.shape[3] <= 2 * LANES
        and translators.shape[2] <= 32
    )
    if tiles:
        return tiled_local(wide, slab, sub, *args)
    return general_local(*args)


def solution(mesh):
    placed = (
        P(("groups", "slab"), "wide", None, "sub", None),
        P(None, "groups", None),
        P(None, ("groups", "wide"), None, None),
        P(),
        P(),
        P(),
        P(None, None, "groups"),
    )
    return jax.shard_map(
        functools.partial(local, mesh.shape["wide"], mesh.shape["slab"], mesh.shape["sub"]),
        mesh=mesh,
        in_specs=placed,
        out_specs=P(("groups", "slab"), "wide", None, "sub", None),
        check_vma=False,
    )
```
